256 devices in a mesh: frame: 32 (over x, y, core), head: 8 (over z).
Axes of the slice: x: 4, y: 4, z: 8, core: 2. Of those that a mesh axis runs over, the one named last changes fastest.
Arguments:
- queries: bfloat16 [1, 16384, 1024], P(None, 'frame', 'head'), may hold values from -256 to 256
- keys: bfloat16 [1, 16384, 1024], P(None, 'frame', 'head'), may hold values from -6 to 6
- values: bfloat16 [1, 16384, 1024], P(None, 'frame', 'head'), may hold values from -6 to 6
- out_weight: bfloat16 [1024, 1024], P('head'), may hold values from -0.1875 to 0.1875
- conv_kernel: bfloat16 [31, 1024], P(None, 'head'), may hold values from -1 to 1
- grad_out: bfloat16 [1024, 1, 16384], P('head', None, 'frame'), may hold values from -6 to 6
- pattern: int32 [1, 32, 7], replicated, may hold values from -1 to 31, as said below
- counts: int32 [1, 32], replicated, may hold values from 1 to 7, as said below
Outputs:
- conv_out: bfloat16 [1024, 1, 16384], P('head', None, 'frame')
- grad_queries: bfloat16 [1, 16384, 1024], P(None, 'frame', 'head')
- grad_keys: bfloat16 [1, 16384, 1024], P(None, 'frame', 'head')
- grad_values: bfloat16 [1, 16384, 1024], P(None, 'frame', 'head')
The draws below stay inside these ranges and needn't reach their ends.
Inputs may be any that keep to these rules, and one draw needn't show every extreme that they name: pattern[s, b, 0] is b; the next entries are the blocks b + o with 0 < |o| <= 3 that lie inside the sequence, each once, in a drawn order; -1 fills the rest. counts[s, b] is at least 1 and at most the number of entries of row b that are not -1; in every sequence some block has 7.
All inputs are finite; a program needn't handle non-finite values.
Results may differ from the reference program's by a relative error of at most 0.035.
Values may be sent and summed in bfloat16 or wider, within the bound.
A program may use at most 64 MiB of HBM per device.

```python
import jax
import jax.numpy as jnp
from jax import lax

HEADS = 16
HEAD_DIM = 64
D = 1024
KERNEL = 31
BLOCK = 512
REACH = 3
MAXK = 7
SEQS = 1
BLOCKS = 32
FRAMES = 16384


def base_keys(key):
    return jnp.clip(jax.random.normal(key, (SEQS, FRAMES, D), jnp.float32), -6.0, 6.0)


def draw_keys(key, part):
    shared = base_keys(key)
    return shared.astype(jnp.bfloat16)


def draw_queries(key, part):
    key = jax.random.fold_in(key, 5)
    drawn = jnp.clip(jax.random.normal(key, (SEQS, FRAMES, D), jnp.float32), -6.0, 6.0)
    return drawn.astype(jnp.bfloat16)


def window_lists(key):
    first, second, third = jax.random.split(key, 3)
    blocks = jnp.arange(BLOCKS, dtype=jnp.int32)
    offsets = jnp.concatenate([jnp.arange(-REACH, 0, dtype=jnp.int32), jnp.arange(1, REACH + 1, dtype=jnp.int32)])
    target = blocks[:, None] + offsets[None, :]
    valid = (target >= 0) & (target < BLOCKS)
    noise = jax.random.randint(first, (SEQS, BLOCKS, 2 * REACH), 0, 4096, dtype=jnp.int32)
    score = jnp.where(valid[None], 1 << 20, 0) + noise * (2 * REACH) + jnp.arange(2 * REACH, dtype=jnp.int32)
    order = jnp.argsort(-score, axis=2)
    entries = jnp.broadcast_to(jnp.where(valid, target, -1)[None], score.shape)
    listed = jnp.take_along_axis(entries, order, axis=2)
    own = jnp.broadcast_to(blocks[None, :, None], (SEQS, BLOCKS, 1))
    pattern = jnp.concatenate([own, listed], axis=2)
    room = 1 + jnp.sum(valid.astype(jnp.int32), axis=1)
    drawn = jnp.maximum(jax.random.randint(second, (SEQS, BLOCKS), 1, MAXK + 1, dtype=jnp.int32), jax.random.randint(third, (SEQS, BLOCKS), 1, MAXK + 1, dtype=jnp.int32))
    counts = jnp.minimum(drawn, room[None, :])
    counts = jnp.where(blocks[None, :] == BLOCKS // 2, MAXK, counts)
    return (pattern.astype(jnp.int32), counts.astype(jnp.int32))


def draw_pattern(key, part):
    pattern, counts = window_lists(key)
    return pattern


def draw_counts(key, part):
    pattern, counts = window_lists(key)
    return counts


def steps_of(stream_key, dims, cuts, least, largest):
    loudness = 1.0
    for axis_at, blocks in cuts:
        steps = jax.random.uniform(jax.random.fold_in(jax.random.fold_in(stream_key, 6), axis_at), (blocks,), jnp.float32, least / len(cuts), largest / len(cuts))
        loudness = loudness * jnp.repeat(jnp.exp(steps), dims[axis_at] // blocks).reshape((-1,) + (1,) * (len(dims) - 1 - axis_at))
    return loudness


def scatter_about(key, shape, scale, limit, cuts=(), held_as=jnp.bfloat16):
    values = jax.random.normal(key, shape, jnp.float32) * scale
    if len(cuts) > 0:
        values = steps_of(key, shape, cuts, -0.22, 0.18) * values
    return jnp.clip(values, min=-limit, max=limit).astype(held_as)


def setup_inputs(seed: int = 0) -> dict:
    splits = jax.random.split(jax.random.key(seed), 9)
    return {
        "queries": draw_queries(jax.random.fold_in(splits[8], 71), 0),
        "keys": draw_keys(jax.random.fold_in(splits[8], 71), 0),
        "values": scatter_about(splits[2], (SEQS, FRAMES, D), 1.0, 6.0, ((1, 32), (2, 8))),
        "out_weight": scatter_about(splits[3], (D, D), D ** -0.5, 0.1875, ((0, 8),)),
        "conv_kernel": scatter_about(splits[4], (KERNEL, D), KERNEL ** -0.5, 1.0, ((1, 8),)),
        "grad_out": scatter_about(splits[5], (D, SEQS, FRAMES), 1.0, 6.0, ((0, 8), (2, 32))),
        "pattern": draw_pattern(jax.random.fold_in(splits[8], 71), 0),
        "counts": draw_counts(jax.random.fold_in(splits[8], 71), 0),
    }


NEGATIVE = -1.0e30


def rounded(value):
    return lax.optimization_barrier(value.astype(jnp.bfloat16)).astype(jnp.float32)


def window_mask(pattern, counts):
    blocks = jnp.arange(BLOCKS, dtype=jnp.int32)
    offsets = jnp.arange(-REACH, REACH + 1, dtype=jnp.int32)
    target = blocks[:, None] + offsets[None, :]
    used = jnp.arange(MAXK, dtype=jnp.int32)[None, None, :] < counts[:, :, None]
    hits = (pattern[:, :, :, None] == target[None, :, None, :]) & used[:, :, :, None]
    return jnp.any(hits, axis=2)


def reference(queries, keys, values, out_weight, conv_kernel, grad_out, pattern, counts):
    scale = HEAD_DIM ** -0.5
    span = 2 * REACH + 1
    mask = window_mask(pattern, counts)
    shape = (SEQS, BLOCKS, BLOCK, HEADS, HEAD_DIM)
    query_all = queries.reshape(shape).astype(jnp.float32)
    padding = jnp.zeros((SEQS, REACH, BLOCK, HEADS, HEAD_DIM), jnp.float32)
    key_pad = jnp.concatenate([padding, keys.reshape(shape).astype(jnp.float32), padding], axis=1)
    value_pad = jnp.concatenate([padding, values.reshape(shape).astype(jnp.float32), padding], axis=1)
    indices = jnp.arange(SEQS * BLOCKS, dtype=jnp.int32)
    anchor = jnp.zeros((), jnp.int32)
    window_size = (1, span, BLOCK, HEADS, HEAD_DIM)

    def block_scores(index):
        seq = (index // BLOCKS).astype(jnp.int32)
        blk = (index % BLOCKS).astype(jnp.int32)
        query = query_all[seq, blk]
        start = (seq, blk, anchor, anchor, anchor)
        key_win = lax.dynamic_slice(key_pad, start, window_size)[0]
        value_win = lax.dynamic_slice(value_pad, start, window_size)[0]
        allowed = mask[seq, blk]
        scores = jnp.einsum("qhd,jkhd->hjqk", query, key_win) * scale
        scores = jnp.where(allowed[None, :, None, None], scores, NEGATIVE)
        return seq, blk, query, key_win, value_win, scores

    def forward(index):
        seq, blk, query, key_win, value_win, scores = block_scores(index)
        peak = jnp.max(scores, axis=(1, 3))
        logsum = peak + jnp.log(jnp.sum(jnp.exp(scores - peak[:, None, :, None]), axis=(1, 3)))
        weights = rounded(jnp.exp(scores - logsum[:, None, :, None]))
        output = jnp.einsum("hjqk,jkhd->qhd", weights, value_win)
        return output.astype(jnp.bfloat16), logsum

    attended, logsums = lax.map(forward, indices)
    attended_flat = attended.reshape(SEQS, FRAMES, D)
    mixed = jnp.einsum("sfa,ac->csf", attended_flat.astype(jnp.float32), out_weight.astype(jnp.float32))
    mixed = mixed.astype(jnp.bfloat16)
    half = KERNEL // 2
    taps = conv_kernel.astype(jnp.float32)
    mixed_pad = jnp.pad(mixed.astype(jnp.float32), ((0, 0), (0, 0), (half, half)))
    grad_pad = jnp.pad(grad_out.astype(jnp.float32), ((0, 0), (0, 0), (half, half)))
    forward_sum = jnp.zeros((D, SEQS, FRAMES), jnp.float32)
    reverse_sum = jnp.zeros((D, SEQS, FRAMES), jnp.float32)
    for tap in range(KERNEL):
        weight = taps[tap][:, None, None]
        forward_sum = forward_sum + weight * mixed_pad[:, :, tap:tap + FRAMES]
        reverse_sum = reverse_sum + weight * grad_pad[:, :, 2 * half - tap:2 * half - tap + FRAMES]
    conv_out = forward_sum.astype(jnp.bfloat16)
    grad_mixed = reverse_sum.astype(jnp.bfloat16)
    grad_attended = jnp.einsum("csf,ac->sfa", grad_mixed.astype(jnp.float32), out_weight.astype(jnp.float32))
    grad_attended = grad_attended.astype(jnp.bfloat16)
    grad_all = grad_attended.reshape(shape).astype(jnp.float32)
    attended_all = attended.reshape(shape).astype(jnp.float32)
    delta_all = jnp.sum(grad_all * attended_all, axis=4)
    logsum_all = logsums.reshape(SEQS, BLOCKS, HEADS, BLOCK)

    def backward(carry, index):
        key_acc, value_acc = carry
        seq, blk, query, key_win, value_win, scores = block_scores(index)
        grad_block = grad_all[seq, blk]
        prob = jnp.exp(scores - logsum_all[seq, blk][:, None, :, None])
        slope = jnp.einsum("qhd,jkhd->hjqk", grad_block, value_win)
        delta = jnp.transpose(delta_all[seq, blk])
        grad_scores = rounded(prob * (slope - delta[:, None, :, None]) * scale)
        grad_query = jnp.einsum("hjqk,jkhd->qhd", grad_scores, key_win)
        grad_key = jnp.einsum("hjqk,qhd->jkhd", grad_scores, query)
        grad_value = jnp.einsum("hjqk,qhd->jkhd", rounded(prob), grad_block)
        start = (seq, blk, anchor, anchor, anchor)
        key_acc = lax.dynamic_update_slice(key_acc, lax.dynamic_slice(key_acc, start, window_size) + grad_key[None], start)
        value_acc = lax.dynamic_update_slice(value_acc, lax.dynamic_slice(value_acc, start, window_size) + grad_value[None], start)
        return (key_acc, value_acc), grad_query.astype(jnp.bfloat16)

    empty = jnp.zeros((SEQS, BLOCKS + 2 * REACH, BLOCK, HEADS, HEAD_DIM), jnp.float32)
    (key_acc, value_acc), grad_query_blocks = lax.scan(backward, (empty, empty), indices)
    grad_queries = grad_query_blocks.reshape(SEQS, FRAMES, D)
    grad_keys = key_acc[:, REACH:REACH + BLOCKS].reshape(SEQS, FRAMES, D).astype(jnp.bfloat16)
    grad_values = value_acc[:, REACH:REACH + BLOCKS].reshape(SEQS, FRAMES, D).astype(jnp.bfloat16)
    return conv_out, grad_queries, grad_keys, grad_values
```

```python
from functools import partial

import jax
import jax.numpy as jnp
from jax import lax
from jax.experimental import pallas as pl
from jax.experimental.pallas import tpu as pltpu
from jax.sharding import PartitionSpec as P

HEAD_DIM = 64
KERNEL = 31
REACH = 3
SPAN = 2 * REACH + 1
HUGE = 1e30
MESH = pl.DeviceIdType.MESH
ORDER = (0, 1, -1, 2, -2, 3, -3)
NEIGHBOURS = (1, -1, 2, -2, 3, -3)
RIM = 16

NT = (((1,), (1,)), ((), ()))
NN = (((1,), (0,)), ((), ()))


def dot(a, b, dims):
    return lax.dot_general(a, b, dims, preferred_element_type=jnp.float32)


def kernel(
    frames,
    heads,
    q_ref,
    k_ref,
    v_ref,
    w_ref,
    t_ref,
    g_ref,
    pat_ref,
    cnt_ref,
    co_ref,
    dq_ref,
    dk_ref,
    dv_ref,
    kv,
    qs,
    do,
    stats,
    gm_all,
    at_all,
    wcol,
    go_t,
    mixed,
    halo,
    pad,
    taps,
    qm,
    km,
    vm,
    dom,
    probs,
    peaks,
    peak,
    total,
    acc,
    delta,
    acc2,
    kv_s,
    kv_r,
    q_s,
    q_r,
    do_s,
    do_r,
    st_s,
    st_r,
    w_s,
    w_r,
    gm_s,
    gm_r,
    at_s,
    at_r,
    h_s,
    h_r,
):
    f = lax.axis_index("frame")
    z = lax.axis_index("head")
    rows, width = q_ref.shape
    R = 256

    def fdev(o):
        return (lax.rem(f + o + frames, frames), z)

    def zrel(i):
        return lax.rem(z + i, heads)

    def remote(src, dst, s, r, dev):
        return pltpu.make_async_remote_copy(
            src_ref=src, dst_ref=dst, send_sem=s, recv_sem=r, device_id=dev, device_id_type=MESH
        )

    barrier = pltpu.get_barrier_semaphore()
    for o in NEIGHBOURS:
        pl.semaphore_signal(barrier, inc=1, device_id=fdev(o), device_id_type=MESH)
    for i in range(1, heads):
        pl.semaphore_signal(barrier, inc=1, device_id=(f, zrel(i)), device_id_type=MESH)

    lane = lax.broadcasted_iota(jnp.int32, (rows, width), 1)
    low = lane < HEAD_DIM

    def split_heads(x, dst):
        x = x.astype(jnp.float32)
        dst[0:rows, :] = jnp.where(low, x, 0.0).astype(jnp.bfloat16)
        dst[rows : 2 * rows, :] = jnp.where(low, 0.0, x).astype(jnp.bfloat16)

    kv[REACH, 0] = k_ref[...]
    kv[REACH, 1] = v_ref[...]
    scaled = (q_ref[...].astype(jnp.float32) * HEAD_DIM**-0.5).astype(jnp.bfloat16)
    qs[REACH] = scaled
    go_t[...] = g_ref[...].T
    taps[0:KERNEL, :] = t_ref[...].astype(jnp.float32)

    pl.semaphore_wait(barrier, len(NEIGHBOURS) + heads - 1)

    def shift(buf, s, r, o):
        return remote(buf.at[REACH], buf.at[REACH - o], s.at[REACH - o], r.at[REACH - o], fdev(o))

    def edge(buf, which, o):
        src = buf.at[pl.ds(rows - RIM, RIM)] if o == 1 else buf.at[pl.ds(0, RIM)]
        side = 0 if o == 1 else 1
        return remote(src, halo.at[which, side], h_s.at[which, side], h_r.at[which, side], fdev(o))

    def spread(buf, s, r, i):
        return remote(buf.at[z], buf.at[z], s.at[i], r.at[z], (f, zrel(i)))

    def spread_arrived(buf, s, r, i):
        src = zrel(i)
        return remote(buf.at[src], buf.at[src], s.at[i], r.at[src], (f, src))

    def weight(i):
        there = zrel(i)
        cols = pl.ds(pl.multiple_of(there * width, width), width)
        return remote(w_ref.at[:, cols], wcol.at[z], w_s.at[i], w_r.at[z], (f, there))

    for o in (1, -1):
        edge(go_t, 0, o).start()
    for o in NEIGHBOURS:
        shift(kv, kv_s, kv_r, o).start()
    for i in range(1, heads):
        weight(i).start()
    for o in NEIGHBOURS:
        shift(qs, q_s, q_r, o).start()
    own_cols = pl.ds(pl.multiple_of(z * width, width), width)
    wcol[z] = w_ref[:, own_cols]

    split_heads(qs[REACH], qm)
    split_heads(k_ref[...], km)
    split_heads(v_ref[...], vm)

    def conv(src, which, flip, out):
        for o in (1, -1):
            edge(src, which, o).wait_recv()
        left = halo[which, 0].astype(jnp.float32)
        right = halo[which, 1].astype(jnp.float32)
        pad[0:RIM, :] = jnp.where(f > 0, left, 0.0)
        pad[RIM : RIM + rows, :] = src[...].astype(jnp.float32)
        pad[RIM + rows : 2 * RIM + rows, :] = jnp.where(f < frames - 1, right, 0.0)
        step = 64
        for c in range(rows // step):
            total_c = jnp.zeros((step, width), jnp.float32)
            for t in range(KERNEL):
                tap = KERNEL - 1 - t if flip else t
                total_c = total_c + taps[tap : tap + 1, :] * pad[c * step + t + 1 : c * step + t + 1 + step, :]
            out(c * step, step, total_c.astype(jnp.bfloat16))

    def to_gm(start, step, value):
        gm_all[z, start : start + step, :] = value

    conv(go_t, 0, True, to_gm)
    for i in range(1, heads):
        spread(gm_all, gm_s, gm_r, i).start()

    def penalty(query_block, key_block):
        inside = (query_block >= 0) & (query_block < frames) & (key_block >= 0) & (key_block < frames)
        safe = lax.rem(query_block + frames, frames)
        number = cnt_ref[0, safe]
        hit = False
        for entry in range(pat_ref.shape[2]):
            hit = hit | ((pat_ref[0, safe, entry] == key_block) & (entry < number))
        return jnp.where(inside & hit, 0.0, HUGE)

    for n, o in enumerate(ORDER):
        slot = REACH + o
        if o != 0:
            shift(kv, kv_s, kv_r, -o).wait_recv()
        pen = penalty(f, f + o)

        def forward(i, carry, slot=slot, first=n == 0, pen=pen):
            at = pl.ds(pl.multiple_of(i * R, R), R)
            s = dot(qm[at, :], kv[slot, 0], NT)
            m = jnp.max(s, axis=1, keepdims=True) - pen
            if not first:
                old = peak[at, :]
                m = jnp.maximum(old, m)
            p = jnp.exp(s - (m + pen))
            l = jnp.sum(p, axis=1, keepdims=True)
            pb = p.astype(jnp.bfloat16)
            probs[slot, at, :] = pb
            pv = dot(pb, kv[slot, 1], NN)
            if not first:
                fade = jnp.exp(old - m)
                l = l + total[at, :] * fade
                pv = pv + acc[at, :] * fade
            peak[at, :] = m
            peaks[slot, at, :] = m
            total[at, :] = l
            acc[at, :] = pv
            return carry

        lax.fori_loop(0, 2 * rows // R, forward, 0)

    inv0 = 1.0 / total[0:rows, :]
    inv1 = 1.0 / total[rows : 2 * rows, :]
    att = jnp.where(low, acc[0:rows, :] * inv0, acc[rows : 2 * rows, :] * inv1).astype(jnp.bfloat16)
    at_all[z] = att
    for i in range(1, heads):
        spread(at_all, at_s, at_r, i).start()

    for i in range(1, heads):
        spread_arrived(gm_all, gm_s, gm_r, i).wait_recv()
    grad = jnp.zeros((rows, width), jnp.float32)
    for i in range(heads):
        grad = grad + dot(gm_all[i], w_ref[:, i * width : (i + 1) * width], NT)
    grad_bf = grad.astype(jnp.bfloat16)
    do[REACH] = grad_bf
    for o in NEIGHBOURS:
        shift(do, do_s, do_r, o).start()
    split_heads(grad_bf, dom)

    product = grad_bf.astype(jnp.float32) * att.astype(jnp.float32)
    delta[0:rows, :] = jnp.sum(jnp.where(low, product, 0.0), axis=1, keepdims=True)
    delta[rows : 2 * rows, :] = jnp.sum(jnp.where(low, 0.0, product), axis=1, keepdims=True)
    logsum = peak[...] + jnp.log(total[...])
    logs = jnp.where(low, logsum[0:rows, :], logsum[rows : 2 * rows, :]).T
    prod_t = product.T
    stats[REACH, 0:1, :] = logs[0:1, :]
    stats[REACH, 1:2, :] = logs[HEAD_DIM : HEAD_DIM + 1, :]
    stats[REACH, 2:3, :] = jnp.sum(prod_t[0:HEAD_DIM, :], axis=0, keepdims=True)
    stats[REACH, 3:4, :] = jnp.sum(prod_t[HEAD_DIM:, :], axis=0, keepdims=True)
    stats[REACH, 4:8, :] = jnp.zeros((4, rows), jnp.float32)
    for o in NEIGHBOURS:
        shift(stats, st_s, st_r, o).start()

    def back_queries(i, carry):
        at = pl.ds(pl.multiple_of(i * R, R), R)
        out = jnp.zeros((R, width), jnp.float32)
        factor = HEAD_DIM**-0.5 / total[at, :]
        for slot in range(SPAN):
            dp = dot(dom[at, :], kv[slot, 1], NT)
            ds = (probs[slot, at, :].astype(jnp.float32) * (dp - delta[at, :])).astype(jnp.bfloat16)
            scale = factor * jnp.exp(peaks[slot, at, :] - peak[at, :])
            out = out + scale * dot(ds, kv[slot, 0], NN)
        acc[at, :] = out
        return carry

    lax.fori_loop(0, 2 * rows // R, back_queries, 0)
    dq_ref[...] = jnp.where(low, acc[0:rows, :], acc[rows : 2 * rows, :]).astype(jnp.bfloat16)

    for i in range(1, heads):
        src = zrel(i)
        remote(w_ref.at[:, own_cols], wcol.at[src], w_s.at[i], w_r.at[src], (f, src)).wait_recv()
    for i in range(1, heads):
        spread_arrived(at_all, at_s, at_r, i).wait_recv()
    mix = jnp.zeros((rows, width), jnp.float32)
    for i in range(heads):
        mix = mix + dot(at_all[i], wcol[i], NN)
    mixed[...] = mix.astype(jnp.bfloat16)
    for o in (1, -1):
        edge(mixed, 1, o).start()

    for n, o in enumerate(ORDER):
        slot = REACH + o
        if o != 0:
            shift(qs, q_s, q_r, -o).wait_recv()
            shift(do, do_s, do_r, -o).wait_recv()
            shift(stats, st_s, st_r, -o).wait_recv()
        pen = penalty(f + o, f)
        for h in range(2):

            def back_keys(i, carry, slot=slot, first=n == 0, pen=pen, h=h):
                at = pl.ds(pl.multiple_of(h * rows + i * R, R), R)
                st = dot(km[at, :], qs[slot], NT)
                pt = jnp.exp(st - (stats[slot, h : h + 1, :] + pen))
                dpt = dot(vm[at, :], do[slot], NT)
                dst = (pt * (dpt - stats[slot, 2 + h : 3 + h, :])).astype(jnp.bfloat16)
                gv = dot(pt.astype(jnp.bfloat16), do[slot], NN)
                gk = dot(dst, qs[slot], NN)
                if not first:
                    gv = gv + acc[at, :]
                    gk = gk + acc2[at, :]
                acc[at, :] = gv
                acc2[at, :] = gk
                return carry

            lax.fori_loop(0, rows // R, back_keys, 0)
    dv_ref[...] = jnp.where(low, acc[0:rows, :], acc[rows : 2 * rows, :]).astype(jnp.bfloat16)
    dk_ref[...] = jnp.where(low, acc2[0:rows, :], acc2[rows : 2 * rows, :]).astype(jnp.bfloat16)

    def to_mixed(start, step, value):
        mixed_out[start : start + step, :] = value

    mixed_out = go_t
    for o in (1, -1):
        edge(go_t, 0, o).wait_send()
    conv(mixed, 1, False, to_mixed)
    co_ref[...] = go_t[...].T

    for o in (1, -1):
        edge(mixed, 1, o).wait_send()
    for o in NEIGHBOURS:
        shift(kv, kv_s, kv_r, o).wait_send()
        shift(qs, q_s, q_r, o).wait_send()
        shift(do, do_s, do_r, o).wait_send()
        shift(stats, st_s, st_r, o).wait_send()
    for i in range(1, heads):
        weight(i).wait_send()
        spread(gm_all, gm_s, gm_r, i).wait_send()
        spread(at_all, at_s, at_r, i).wait_send()


def on_device(queries, keys, values, out_weight, conv_kernel, grad_out, pattern, counts):
    _, rows, width = queries.shape
    frames, heads = lax.axis_size("frame"), lax.axis_size("head")
    bf, f32 = jnp.bfloat16, jnp.float32
    block = (rows, width)
    vmem = pl.BlockSpec(memory_space=pltpu.VMEM)
    smem = pl.BlockSpec(memory_space=pltpu.SMEM)
    dma = pltpu.SemaphoreType.DMA
    conv_out, dq, dk, dv = pl.pallas_call(
        partial(kernel, frames, heads),
        out_shape=[
            jax.ShapeDtypeStruct((width, rows), bf),
            jax.ShapeDtypeStruct(block, bf),
            jax.ShapeDtypeStruct(block, bf),
            jax.ShapeDtypeStruct(block, bf),
        ],
        in_specs=[vmem] * 6 + [smem] * 2,
        out_specs=[vmem] * 4,
        scratch_shapes=[
            pltpu.VMEM((SPAN, 2) + block, bf),
            pltpu.VMEM((SPAN,) + block, bf),
            pltpu.VMEM((SPAN,) + block, bf),
            pltpu.VMEM((SPAN, 8, rows), f32),
            pltpu.VMEM((heads,) + block, bf),
            pltpu.VMEM((heads,) + block, bf),
            pltpu.VMEM((heads, width, width), bf),
            pltpu.VMEM(block, bf),
            pltpu.VMEM(block, bf),
            pltpu.VMEM((2, 2, RIM, width), bf),
            pltpu.VMEM((rows + 2 * RIM, width), f32),
            pltpu.VMEM((32, width), f32),
            pltpu.VMEM((2 * rows, width), bf),
            pltpu.VMEM((2 * rows, width), bf),
            pltpu.VMEM((2 * rows, width), bf),
            pltpu.VMEM((2 * rows, width), bf),
            pltpu.VMEM((SPAN, 2 * rows, rows), bf),
            pltpu.VMEM((SPAN, 2 * rows, 1), f32),
            pltpu.VMEM((2 * rows, 1), f32),
            pltpu.VMEM((2 * rows, 1), f32),
            pltpu.VMEM((2 * rows, width), f32),
            pltpu.VMEM((2 * rows, 1), f32),
            pltpu.VMEM((2 * rows, width), f32),
            dma((SPAN,)),
            dma((SPAN,)),
            dma((SPAN,)),
            dma((SPAN,)),
            dma((SPAN,)),
            dma((SPAN,)),
            dma((SPAN,)),
            dma((SPAN,)),
            dma((heads,)),
            dma((heads,)),
            dma((heads,)),
            dma((heads,)),
            dma((heads,)),
            dma((heads,)),
            dma((2, 2)),
            dma((2, 2)),
        ],
        compiler_params=pltpu.CompilerParams(
            collective_id=0, has_side_effects=True, vmem_limit_bytes=48 * 1024 * 1024
        ),
    )(
        queries.reshape(block),
        keys.reshape(block),
        values.reshape(block),
        out_weight,
        conv_kernel,
        grad_out.reshape(width, rows),
        pattern,
        counts,
    )
    return (
        conv_out.reshape(grad_out.shape),
        dq.reshape(queries.shape),
        dk.reshape(keys.shape),
        dv.reshape(values.shape),
    )


def solution(mesh):
    return jax.shard_map(
        on_device,
        mesh=mesh,
        in_specs=(
            P(None, "frame", "head"),
            P(None, "frame", "head"),
            P(None, "frame", "head"),
            P("head", None),
            P(None, "head"),
            P("head", None, "frame"),
            P(),
            P(),
        ),
        out_specs=(
            P("head", None, "frame"),
            P(None, "frame", "head"),
            P(None, "frame", "head"),
            P(None, "frame", "head"),
        ),
        check_vma=False,
    )
```

```python
from functools import partial, reduce

import jax
import jax.numpy as jnp
from jax import lax
from jax.experimental import pallas as pl
from jax.experimental.pallas import tpu as pltpu
from jax.sharding import PartitionSpec as P

HEAD_DIM = 64
KERNEL = 31
SPAN = 7
HUGE = 1e30
MESH = pl.DeviceIdType.MESH
RIM = 16
HOPS = 4

NT = (((1,), (1,)), ((), ()))
NN = (((1,), (0,)), ((), ()))

OWN, PAIR, UP, DOWN, PAIR_UP, PAIR_DOWN, FAR = range(SPAN)
GROUPS = ((OWN,), (PAIR,), (UP, DOWN), (PAIR_UP, PAIR_DOWN), (FAR,))


def dot(a, b, dims):
    return lax.dot_general(a, b, dims, preferred_element_type=jnp.float32)


def remote(src, dst, s, r, dev):
    return pltpu.make_async_remote_copy(
        src_ref=src, dst_ref=dst, send_sem=s, recv_sem=r, device_id=dev, device_id_type=MESH
    )


def kernel(
    frames,
    heads,
    q_hbm,
    k_hbm,
    v_hbm,
    w_hbm,
    t_hbm,
    g_hbm,
    pat_ref,
    cnt_ref,
    co_hbm,
    dq_hbm,
    dk_hbm,
    dv_hbm,
    w_ref,
    t_ref,
    g_ref,
    co_ref,
    dq_ref,
    dk_ref,
    dv_ref,
    kv,
    kt,
    vt,
    qs,
    do,
    stats,
    gm_all,
    at_all,
    wcol,
    wcol_t,
    go_t,
    mixed,
    conv_tmp,
    halo,
    pad,
    taps,
    qmt,
    dmt,
    km,
    vm,
    probs,
    peaks,
    peak,
    total,
    acc,
    gk_acc,
    gv_acc,
    in_s,
    out_s,
    kv_s,
    kv_r,
    q_s,
    q_r,
    do_s,
    do_r,
    st_s,
    st_r,
    w_s,
    w_r,
    gm_s,
    gm_r,
    at_s,
    at_r,
    h_s,
    h_r,
):
    f = lax.axis_index("frame")
    z = lax.axis_index("head")
    rows, width = kv.shape[2], kv.shape[3]
    odd = lax.rem(f, 2)
    sign = 2 * odd - 1

    def fdev(o):
        return (lax.rem(f + o + frames, frames), z)

    def zrel(i):
        return lax.rem(z + i + heads, heads)

    def part(index, size=width, start=0):
        return pl.ds(pl.multiple_of(index * width + start, size), size)

    offsets = (0, -sign, 2, -2, 2 - sign, -2 - sign, 3 * sign)

    loads = [
        pltpu.make_async_copy(src, dst, in_s.at[n])
        for n, (src, dst) in enumerate(
            (
                (g_hbm, g_ref),
                (k_hbm, kv.at[OWN, 0]),
                (v_hbm, kv.at[OWN, 1]),
                (q_hbm, qs.at[OWN]),
                (t_hbm, t_ref),
                (w_hbm, w_ref),
            )
        )
    ]
    for load in loads:
        load.start()

    barrier = pltpu.get_barrier_semaphore()
    for o in offsets[1:]:
        pl.semaphore_signal(barrier, inc=1, device_id=fdev(o), device_id_type=MESH)
    for i in range(1, heads):
        pl.semaphore_signal(barrier, inc=1, device_id=(f, zrel(i)), device_id_type=MESH)

    def route(buf, s, r, role):
        src, o = {
            PAIR: (OWN, -sign),
            DOWN: (OWN, 2),
            UP: (OWN, -2),
            PAIR_UP: (UP, -sign),
            PAIR_DOWN: (DOWN, -sign),
            FAR: (UP + odd, sign),
        }[role]
        return remote(buf.at[src], buf.at[role], s.at[role], r.at[role], fdev(o))

    FIRST, SECOND = (UP, DOWN, PAIR), (FAR, PAIR_UP, PAIR_DOWN)

    def direct(role):
        o = {
            PAIR: -sign,
            DOWN: 2,
            UP: -2,
            PAIR_DOWN: 2 - sign,
            PAIR_UP: -2 - sign,
            FAR: 3 * sign,
        }[role]
        return remote(stats.at[OWN], stats.at[role], st_s.at[role], st_r.at[role], fdev(o))

    def edge(buf, which, o):
        src = buf.at[pl.ds(rows - RIM, RIM)] if o == 1 else buf.at[pl.ds(0, RIM)]
        side = 0 if o == 1 else 1
        return remote(src, halo.at[which, side], h_s.at[which, side], h_r.at[which, side], fdev(o))

    def weight(i):
        there = zrel(i)
        return remote(w_ref.at[:, part(there)], wcol.at[z], w_s.at[i], w_r.at[z], (f, there))

    def hop(buf, s, r, way, k, arrived=False):
        back = k if arrived else k - 1
        origin = zrel(-back if way == 0 else back)
        half = width // 2
        at = part(origin) if k < HOPS else part(origin, half, half * way)
        return remote(
            buf.at[at], buf.at[at], s.at[way, k - 1], r.at[way, k - 1], (f, zrel(1 if way == 0 else -1))
        )

    def pass_on(buf, s, r, k):
        for way in range(2):
            if k > 1:
                hop(buf, s, r, way, k - 1, True).wait_recv()
            hop(buf, s, r, way, k).start()

    def penalty(query_block, key_block):
        inside = (query_block >= 0) & (query_block < frames) & (key_block >= 0) & (key_block < frames)
        safe = lax.rem(query_block + frames, frames)
        number = cnt_ref[0, safe]
        hit = False
        for entry in range(pat_ref.shape[2]):
            hit = hit | ((pat_ref[0, safe, entry] == key_block) & (entry < number))
        return jnp.where(inside & hit, 0.0, HUGE)

    def conv(src, which, flip, out):
        pad[RIM : RIM + rows, :] = src[...].astype(jnp.float32)
        for o in (1, -1):
            edge(src, which, o).wait_recv()
        left = halo[which, 0].astype(jnp.float32)
        right = halo[which, 1].astype(jnp.float32)
        pad[0:RIM, :] = jnp.where(f > 0, left, 0.0)
        pad[RIM + rows : 2 * RIM + rows, :] = jnp.where(f < frames - 1, right, 0.0)
        step = 64
        for c in range(rows // step):
            total_c = jnp.zeros((step, width), jnp.float32)
            for t in range(KERNEL):
                tap = KERNEL - 1 - t if flip else t
                total_c = total_c + taps[tap : tap + 1, :] * pad[c * step + t + 1 : c * step + t + 1 + step, :]
            out[c * step : c * step + step, :] = total_c.astype(jnp.bfloat16)

    def head_columns(x, dst):
        dst[0:HEAD_DIM, 0:rows] = x[0:HEAD_DIM, :]
        dst[HEAD_DIM:width, rows : 2 * rows] = x[HEAD_DIM:width, :]
        dst[0:HEAD_DIM, rows : 2 * rows] = jnp.zeros((HEAD_DIM, rows), jnp.bfloat16)
        dst[HEAD_DIM:width, 0:rows] = jnp.zeros((HEAD_DIM, rows), jnp.bfloat16)

    low = lax.broadcasted_iota(jnp.int32, (rows, width), 1) < HEAD_DIM

    def head_rows(x, dst):
        x = x.astype(jnp.float32)
        dst[0:rows, :] = jnp.where(low, x, 0.0).astype(jnp.bfloat16)
        dst[rows : 2 * rows, :] = jnp.where(low, 0.0, x).astype(jnp.bfloat16)

    def by_head(row):
        return jnp.concatenate(
            [
                jnp.broadcast_to(row[:, 0:rows], (HEAD_DIM, rows)),
                jnp.broadcast_to(row[:, rows : 2 * rows], (HEAD_DIM, rows)),
            ],
            axis=0,
        )

    def forward(group):
        roles = GROUPS[group]
        for role in roles:
            vt[role] = kv[role, 1].T
        scores = [dot(kv[role, 0], qmt[...], NN) for role in roles]
        pens = [penalty(f, f + offsets[role]) for role in roles]
        m = reduce(
            jnp.maximum, [jnp.max(s, axis=0, keepdims=True) - pen for s, pen in zip(scores, pens)]
        )
        if group > 0:
            old = peak[...]
            m = jnp.maximum(old, m)
        sums, outs = [], []
        for role, s, pen in zip(roles, scores, pens):
            p = jnp.exp(s - (m + pen))
            sums.append(jnp.sum(p, axis=0, keepdims=True))
            weights = p.astype(jnp.bfloat16)
            probs[role] = weights
            outs.append(
                jnp.concatenate(
                    [
                        dot(vt[role, 0:HEAD_DIM, :], weights[:, 0:rows], NN),
                        dot(vt[role, HEAD_DIM:width, :], weights[:, rows : 2 * rows], NN),
                    ],
                    axis=0,
                )
            )
        row_sum, out = reduce(jnp.add, sums), reduce(jnp.add, outs)
        if group > 0:
            fade = jnp.exp(old - m)
            row_sum = row_sum + total[...] * fade
            out = out + acc[...] * by_head(fade)
        peak[...] = m
        peaks[group] = m
        total[...] = row_sum
        acc[...] = out

    def back_queries(h):
        cols = slice(h * rows, h * rows + rows)
        feats = slice(h * HEAD_DIM, (h + 1) * HEAD_DIM)
        out = jnp.zeros((HEAD_DIM, rows), jnp.float32)
        factor = HEAD_DIM**-0.5 / total[:, cols]
        delta = stats[OWN, 2 + h : 3 + h, :]
        for group, roles in enumerate(GROUPS):
            scale = factor * jnp.exp(peaks[group, :, cols] - peak[:, cols])
            for role in roles:
                dp = dot(kv[role, 1], dmt[:, cols], NN)
                ds = (probs[role, :, cols].astype(jnp.float32) * (dp - delta)).astype(jnp.bfloat16)
                out = out + scale * dot(kt[role, feats, :], ds, NN)
        acc[feats, :] = out

    def back_keys(role):
        pen = penalty(f + offsets[role], f)
        for h in range(2):
            at = slice(h * rows, h * rows + rows)
            st = dot(km[at, :], qs[role], NT)
            pt = jnp.exp(st - (stats[role, h : h + 1, :] + pen))
            dpt = dot(vm[at, :], do[role], NT)
            dst = (pt * (dpt - stats[role, 2 + h : 3 + h, :])).astype(jnp.bfloat16)
            gv = dot(pt.astype(jnp.bfloat16), do[role], NN)
            gk = dot(dst, qs[role], NN)
            if role != OWN:
                gv = gv + gv_acc[at, :]
                gk = gk + gk_acc[at, :]
            gv_acc[at, :] = gv
            gk_acc[at, :] = gk

    loads[0].wait()
    go_t[...] = g_ref[...].T
    loads[1].wait()
    loads[2].wait()
    pl.semaphore_wait(barrier, SPAN - 1 + heads - 1)
    for o in (1, -1):
        edge(go_t, 0, o).start()
    for role in FIRST:
        route(kv, kv_s, kv_r, role).start()
    loads[5].wait()
    for i in range(1, heads):
        weight(i).start()
    loads[3].wait()
    loads[4].wait()
    taps[0:KERNEL, :] = t_ref[...].astype(jnp.float32)
    qs[OWN] = (qs[OWN].astype(jnp.float32) * HEAD_DIM**-0.5).astype(jnp.bfloat16)
    head_columns(qs[OWN].T, qmt)

    conv(go_t, 0, True, conv_tmp)
    gm_all[part(z), :] = conv_tmp[...].T
    pass_on(gm_all, gm_s, gm_r, 1)

    forward(0)
    route(kv, kv_s, kv_r, PAIR).wait_recv()
    forward(1)
    route(kv, kv_s, kv_r, UP).wait_recv()
    route(kv, kv_s, kv_r, DOWN).wait_recv()
    for role in SECOND:
        route(kv, kv_s, kv_r, role).start()
    for role in FIRST:
        route(qs, q_s, q_r, role).start()
    forward(2)
    pass_on(gm_all, gm_s, gm_r, 2)
    route(kv, kv_s, kv_r, PAIR_UP).wait_recv()
    route(kv, kv_s, kv_r, PAIR_DOWN).wait_recv()
    forward(3)
    route(kv, kv_s, kv_r, FAR).wait_recv()
    forward(4)

    attended = (acc[...] * by_head(1.0 / total[...])).astype(jnp.bfloat16)
    at_all[part(z), :] = attended
    pass_on(gm_all, gm_s, gm_r, 3)
    pass_on(at_all, at_s, at_r, 1)

    head_rows(kv[OWN, 0], km)
    head_rows(kv[OWN, 1], vm)
    for role in range(SPAN):
        kt[role] = kv[role, 0].T
    logsum = peak[...] + jnp.log(total[...])
    stats[OWN, 0:1, :] = logsum[:, 0:rows]
    stats[OWN, 1:2, :] = logsum[:, rows : 2 * rows]
    stats[OWN, 4:8, :] = jnp.zeros((4, rows), jnp.float32)
    wcol[z] = w_ref[:, part(z)]
    route(qs, q_s, q_r, UP).wait_recv()
    route(qs, q_s, q_r, DOWN).wait_recv()
    for role in SECOND:
        route(qs, q_s, q_r, role).start()
    pass_on(gm_all, gm_s, gm_r, 4)
    for i in range(1, heads):
        src = zrel(i)
        remote(w_ref.at[:, part(z)], wcol.at[src], w_s.at[i], w_r.at[src], (f, src)).wait_recv()
    for i in range(heads):
        wcol_t[:, i * width : (i + 1) * width] = wcol[i].T
    for way in range(2):
        hop(gm_all, gm_s, gm_r, way, HOPS, True).wait_recv()

    grad_t = dot(w_ref[...], gm_all[...], NN).astype(jnp.bfloat16)
    do[OWN] = grad_t.T
    for role in FIRST:
        route(do, do_s, do_r, role).start()
    product = grad_t.astype(jnp.float32) * attended.astype(jnp.float32)
    stats[OWN, 2:3, :] = jnp.sum(product[0:HEAD_DIM, :], axis=0, keepdims=True)
    stats[OWN, 3:4, :] = jnp.sum(product[HEAD_DIM:width, :], axis=0, keepdims=True)
    for role in range(1, SPAN):
        direct(role).start()
    head_columns(grad_t, dmt)

    pass_on(at_all, at_s, at_r, 2)
    back_queries(0)
    pass_on(at_all, at_s, at_r, 3)
    route(do, do_s, do_r, UP).wait_recv()
    route(do, do_s, do_r, DOWN).wait_recv()
    for role in SECOND:
        route(do, do_s, do_r, role).start()
    back_queries(1)
    dq_ref[...] = acc[...].T.astype(jnp.bfloat16)
    stores = [
        pltpu.make_async_copy(src, dst, out_s.at[n])
        for n, (src, dst) in enumerate(
            ((dq_ref, dq_hbm), (dk_ref, dk_hbm), (dv_ref, dv_hbm), (co_ref, co_hbm))
        )
    ]
    stores[0].start()
    pass_on(at_all, at_s, at_r, 4)
    back_keys(OWN)

    def keys_of(role):
        if role in (PAIR, PAIR_UP, PAIR_DOWN, FAR):
            route(qs, q_s, q_r, role).wait_recv()
            route(do, do_s, do_r, role).wait_recv()
        direct(role).wait_recv()
        back_keys(role)

    keys_of(PAIR)
    keys_of(UP)
    keys_of(DOWN)

    for way in range(2):
        hop(at_all, at_s, at_r, way, HOPS, True).wait_recv()
    mixed[...] = dot(wcol_t[...], at_all[...], NN).T.astype(jnp.bfloat16)
    for o in (1, -1):
        edge(mixed, 1, o).start()

    keys_of(PAIR_UP)
    keys_of(PAIR_DOWN)
    keys_of(FAR)
    dv_ref[...] = jnp.where(low, gv_acc[0:rows, :], gv_acc[rows : 2 * rows, :]).astype(jnp.bfloat16)
    dk_ref[...] = jnp.where(low, gk_acc[0:rows, :], gk_acc[rows : 2 * rows, :]).astype(jnp.bfloat16)
    stores[1].start()
    stores[2].start()

    conv(mixed, 1, False, conv_tmp)
    co_ref[...] = conv_tmp[...].T
    stores[3].start()

    for o in (1, -1):
        edge(go_t, 0, o).wait_send()
        edge(mixed, 1, o).wait_send()
    for role in range(1, SPAN):
        route(kv, kv_s, kv_r, role).wait_send()
        route(qs, q_s, q_r, role).wait_send()
        route(do, do_s, do_r, role).wait_send()
        direct(role).wait_send()
    for i in range(1, heads):
        weight(i).wait_send()
    for k in range(1, HOPS + 1):
        for way in range(2):
            hop(gm_all, gm_s, gm_r, way, k).wait_send()
            hop(at_all, at_s, at_r, way, k).wait_send()
    for store in stores:
        store.wait()


def on_device(queries, keys, values, out_weight, conv_kernel, grad_out, pattern, counts):
    _, rows, width = queries.shape
    frames, heads = lax.axis_size("frame"), lax.axis_size("head")
    bf, f32 = jnp.bfloat16, jnp.float32
    block, tall = (rows, width), (width, rows)
    hbm = pl.BlockSpec(memory_space=pltpu.HBM)
    smem = pl.BlockSpec(memory_space=pltpu.SMEM)
    dma = pltpu.SemaphoreType.DMA
    conv_out, dq, dk, dv = pl.pallas_call(
        partial(kernel, frames, heads),
        out_shape=[
            jax.ShapeDtypeStruct(tall, bf),
            jax.ShapeDtypeStruct(block, bf),
            jax.ShapeDtypeStruct(block, bf),
            jax.ShapeDtypeStruct(block, bf),
        ],
        in_specs=[hbm] * 6 + [smem] * 2,
        out_specs=[hbm] * 4,
        scratch_shapes=[
            pltpu.VMEM(out_weight.shape, bf),
            pltpu.VMEM(conv_kernel.shape, bf),
            pltpu.VMEM(tall, bf),
            pltpu.VMEM(tall, bf),
            pltpu.VMEM(block, bf),
            pltpu.VMEM(block, bf),
            pltpu.VMEM(block, bf),
            pltpu.VMEM((SPAN, 2) + block, bf),
            pltpu.VMEM((SPAN,) + tall, bf),
            pltpu.VMEM((SPAN,) + tall, bf),
            pltpu.VMEM((SPAN,) + block, bf),
            pltpu.VMEM((SPAN,) + block, bf),
            pltpu.VMEM((SPAN, 8, rows), f32),
            pltpu.VMEM((heads * width, rows), bf),
            pltpu.VMEM((heads * width, rows), bf),
            pltpu.VMEM((heads, width, width), bf),
            pltpu.VMEM((width, heads * width), bf),
            pltpu.VMEM(block, bf),
            pltpu.VMEM(block, bf),
            pltpu.VMEM(block, bf),
            pltpu.VMEM((2, 2, RIM, width), bf),
            pltpu.VMEM((rows + 2 * RIM, width), f32),
            pltpu.VMEM((32, width), f32),
            pltpu.VMEM((width, 2 * rows), bf),
            pltpu.VMEM((width, 2 * rows), bf),
            pltpu.VMEM((2 * rows, width), bf),
            pltpu.VMEM((2 * rows, width), bf),
            pltpu.VMEM((SPAN, rows, 2 * rows), bf),
            pltpu.VMEM((len(GROUPS), 1, 2 * rows), f32),
            pltpu.VMEM((1, 2 * rows), f32),
            pltpu.VMEM((1, 2 * rows), f32),
            pltpu.VMEM(tall, f32),
            pltpu.VMEM((2 * rows, width), f32),
            pltpu.VMEM((2 * rows, width), f32),
            dma((6,)),
            dma((4,)),
        ]
        + [dma((SPAN,))] * 8
        + [dma((heads,))] * 2
        + [dma((2, HOPS))] * 4
        + [dma((2, 2))] * 2,
        compiler_params=pltpu.CompilerParams(
            collective_id=0, has_side_effects=True, vmem_limit_bytes=56 * 1024 * 1024
        ),
    )(
        queries.reshape(block),
        keys.reshape(block),
        values.reshape(block),
        out_weight,
        conv_kernel,
        grad_out.reshape(width, rows),
        pattern,
        counts,
    )
    return (
        conv_out.reshape(grad_out.shape),
        dq.reshape(queries.shape),
        dk.reshape(keys.shape),
        dv.reshape(values.shape),
    )


def solution(mesh):
    return jax.shard_map(
        on_device,
        mesh=mesh,
        in_specs=(
            P(None, "frame", "head"),
            P(None, "frame", "head"),
            P(None, "frame", "head"),
            P("head", None),
            P(None, "head"),
            P("head", None, "frame"),
            P(),
            P(),
        ),
        out_specs=(
            P("head", None, "frame"),
            P(None, "frame", "head"),
            P(None, "frame", "head"),
            P(None, "frame", "head"),
        ),
        check_vma=False,
    )
```

```python
from functools import partial, reduce

import jax
import jax.numpy as jnp
from jax import lax
from jax.experimental import pallas as pl
from jax.experimental.pallas import tpu as pltpu
from jax.sharding import PartitionSpec as P

HEAD_DIM = 64
KERNEL = 31
SPAN = 7
HUGE = 1e30
MESH = pl.DeviceIdType.MESH
RIM = 16
MAIL = 64

NT = (((1,), (1,)), ((), ()))
NN = (((1,), (0,)), ((), ()))

OWN, PAIR, UP, DOWN, PAIR_UP, PAIR_DOWN, FAR = range(SPAN)
GROUPS = ((OWN,), (PAIR,), (UP, DOWN), (PAIR_UP, PAIR_DOWN), (FAR,))


def dot(a, b, dims):
    return lax.dot_general(a, b, dims, preferred_element_type=jnp.float32)


def remote(src, dst, s, r, dev):
    return pltpu.make_async_remote_copy(
        src_ref=src, dst_ref=dst, send_sem=s, recv_sem=r, device_id=dev, device_id_type=MESH
    )


def kernel(
    frames,
    heads,
    q_hbm,
    k_hbm,
    v_hbm,
    w_hbm,
    t_hbm,
    g_hbm,
    pat_ref,
    cnt_ref,
    co_ref,
    dq_ref,
    dk_ref,
    dv_ref,
    w_ref,
    t_ref,
    g_ref,
    kv,
    kt,
    vt,
    qs,
    do,
    stats,
    g_all,
    at_all,
    mail,
    mail_all,
    ends,
    rim,
    rim_all,
    wcol,
    wcol_t,
    conv_tmp,
    pad,
    taps,
    grad_acc,
    qmt,
    dmt,
    km,
    vm,
    probs,
    peaks,
    peak,
    total,
    acc,
    gk_acc,
    gv_acc,
    in_s,
    kv_s,
    kv_r,
    q_s,
    q_r,
    do_s,
    do_r,
    st_s,
    st_r,
    w_s,
    w_r,
    g_s,
    g_r,
    at_s,
    at_r,
    m_s,
    m_r,
    e_s,
    e_r,
    h_s,
    h_r,
):
    f = lax.axis_index("frame")
    z = lax.axis_index("head")
    rows, width = kv.shape[2], kv.shape[3]
    odd = lax.rem(f, 2)
    sign = 2 * odd - 1

    def fdev(o):
        return (lax.rem(f + o + frames, frames), z)

    def zrel(i):
        return lax.rem(z + i + heads, heads)

    def part(index, size=width, start=0):
        return pl.ds(pl.multiple_of(index * width + start, size), size)

    offsets = (0, -sign, 2, -2, 2 - sign, -2 - sign, 3 * sign)

    loads = [
        pltpu.make_async_copy(src, dst, in_s.at[n])
        for n, (src, dst) in enumerate(
            (
                (g_hbm, g_ref),
                (k_hbm, kv.at[OWN, 0]),
                (v_hbm, kv.at[OWN, 1]),
                (q_hbm, qs.at[OWN]),
                (t_hbm, t_ref),
                (w_hbm, w_ref),
            )
        )
    ]
    for load in loads:
        load.start()

    barrier = pltpu.get_barrier_semaphore()
    for o in offsets[1:]:
        pl.semaphore_signal(barrier, inc=1, device_id=fdev(o), device_id_type=MESH)
    for i in range(1, heads):
        pl.semaphore_signal(barrier, inc=1, device_id=(f, zrel(i)), device_id_type=MESH)

    def route(buf, s, r, role):
        src, o = {
            PAIR: (OWN, -sign),
            DOWN: (OWN, 2),
            UP: (OWN, -2),
            FAR: (OWN, 3 * sign),
            PAIR_UP: (UP, -sign),
            PAIR_DOWN: (DOWN, -sign),
        }[role]
        return remote(buf.at[src], buf.at[role], s.at[role], r.at[role], fdev(o))

    FIRST, SECOND = (UP, DOWN, PAIR, FAR), (PAIR_UP, PAIR_DOWN)

    def direct(role):
        o = {
            PAIR: -sign,
            DOWN: 2,
            UP: -2,
            PAIR_DOWN: 2 - sign,
            PAIR_UP: -2 - sign,
            FAR: 3 * sign,
        }[role]
        return remote(stats.at[OWN], stats.at[role], st_s.at[role], st_r.at[role], fdev(o))

    def edge(src, dst, which, o):
        side = 0 if o == 1 else 1
        at = pl.ds(side * RIM, RIM)
        return remote(src, dst.at[at], h_s.at[which, side], h_r.at[which, side], fdev(o))

    def post(src, dst, s, r, i):
        return remote(src, dst.at[z], s.at[i], r.at[z], (f, zrel(i)))

    def posted(src, dst, s, r, i):
        origin = zrel(i)
        return remote(src, dst.at[origin], s.at[i], r.at[origin], (f, origin))

    def weight(i):
        there = zrel(i)
        return remote(w_ref.at[:, part(there)], wcol.at[z], w_s.at[i], w_r.at[z], (f, there))

    HOPS = ((0, 2), (0, -2), (0, 1), (0, -1), (-2, 1), (2, -1), (-2, 2), (2, -2))

    def hop(buf, s, r, n, arrived=False):
        origin, target = HOPS[n]
        slot = zrel(origin - target if arrived else origin)
        block = buf.at[slot]
        if n >= 6:
            half = buf.shape[1] // 2
            block = buf.at[slot, pl.ds(half * (n - 6), half)]
        return remote(block, block, s.at[n], r.at[n], (f, zrel(target)))

    def hops(buf, s, r, which):
        for n in which:
            hop(buf, s, r, n).start()

    def arrive(buf, s, r, which):
        for n in which:
            hop(buf, s, r, n, True).wait_recv()

    def penalty(query_block, key_block):
        inside = (query_block >= 0) & (query_block < frames) & (key_block >= 0) & (key_block < frames)
        safe = lax.rem(query_block + frames, frames)
        number = cnt_ref[0, safe]
        hit = False
        for entry in range(pat_ref.shape[0]):
            hit = hit | ((pat_ref[entry, 0, safe] == key_block) & (entry < number))
        return jnp.where(inside & hit, 0.0, HUGE)

    def conv(left, right, flip, out):
        pad[0:RIM, :] = jnp.where(f > 0, left.astype(jnp.float32), 0.0)
        pad[RIM + rows : 2 * RIM + rows, :] = jnp.where(f < frames - 1, right.astype(jnp.float32), 0.0)
        step = 64
        for c in range(rows // step):
            total_c = jnp.zeros((step, width), jnp.float32)
            for t in range(KERNEL):
                tap = KERNEL - 1 - t if flip else t
                total_c = total_c + taps[tap : tap + 1, :] * pad[c * step + t + 1 : c * step + t + 1 + step, :]
            out[c * step : c * step + step, :] = total_c.astype(jnp.bfloat16)

    def conv_group(group):
        pad[RIM : RIM + rows, :] = g_all[group].astype(jnp.float32)
        taps[...] = mail_all[group, 2 * RIM : MAIL, :].astype(jnp.float32)
        conv(mail_all[group, 0:RIM, :], mail_all[group, RIM : 2 * RIM, :], True, conv_tmp)
        grad_acc[...] += dot(w_ref[:, part(group)], conv_tmp[...], NT)

    def head_columns(x, dst):
        dst[0:HEAD_DIM, 0:rows] = x[0:HEAD_DIM, :]
        dst[HEAD_DIM:width, rows : 2 * rows] = x[HEAD_DIM:width, :]
        dst[0:HEAD_DIM, rows : 2 * rows] = jnp.zeros((HEAD_DIM, rows), jnp.bfloat16)
        dst[HEAD_DIM:width, 0:rows] = jnp.zeros((HEAD_DIM, rows), jnp.bfloat16)

    low = lax.broadcasted_iota(jnp.int32, (rows, width), 1) < HEAD_DIM

    def head_rows(x, dst):
        x = x.astype(jnp.float32)
        dst[0:rows, :] = jnp.where(low, x, 0.0).astype(jnp.bfloat16)
        dst[rows : 2 * rows, :] = jnp.where(low, 0.0, x).astype(jnp.bfloat16)

    def by_head(row):
        return jnp.concatenate(
            [
                jnp.broadcast_to(row[:, 0:rows], (HEAD_DIM, rows)),
                jnp.broadcast_to(row[:, rows : 2 * rows], (HEAD_DIM, rows)),
            ],
            axis=0,
        )

    def forward(group):
        roles = GROUPS[group]
        for role in roles:
            vt[role] = kv[role, 1].T
        scores = [dot(kv[role, 0], qmt[...], NN) for role in roles]
        pens = [penalty(f, f + offsets[role]) for role in roles]
        m = reduce(
            jnp.maximum, [jnp.max(s, axis=0, keepdims=True) - pen for s, pen in zip(scores, pens)]
        )
        if group > 0:
            old = peak[...]
            m = jnp.maximum(old, m)
        sums, outs = [], []
        for role, s, pen in zip(roles, scores, pens):
            p = jnp.exp(s - (m + pen))
            sums.append(jnp.sum(p, axis=0, keepdims=True))
            weights = p.astype(jnp.bfloat16)
            probs[role] = weights
            outs.append(
                jnp.concatenate(
                    [
                        dot(vt[role, 0:HEAD_DIM, :], weights[:, 0:rows], NN),
                        dot(vt[role, HEAD_DIM:width, :], weights[:, rows : 2 * rows], NN),
                    ],
                    axis=0,
                )
            )
        row_sum, out = reduce(jnp.add, sums), reduce(jnp.add, outs)
        if group > 0:
            fade = jnp.exp(old - m)
            row_sum = row_sum + total[...] * fade
            out = out + acc[...] * by_head(fade)
        peak[...] = m
        peaks[group] = m
        total[...] = row_sum
        acc[...] = out

    def back_queries(h):
        cols = slice(h * rows, h * rows + rows)
        feats = slice(h * HEAD_DIM, (h + 1) * HEAD_DIM)
        out = jnp.zeros((HEAD_DIM, rows), jnp.float32)
        factor = HEAD_DIM**-0.5 / total[:, cols]
        delta = stats[OWN, 2 + h : 3 + h, :]
        for group, roles in enumerate(GROUPS):
            scale = factor * jnp.exp(peaks[group, :, cols] - peak[:, cols])
            for role in roles:
                dp = dot(kv[role, 1], dmt[:, cols], NN)
                ds = (probs[role, :, cols].astype(jnp.float32) * (dp - delta)).astype(jnp.bfloat16)
                out = out + scale * dot(kt[role, feats, :], ds, NN)
        acc[feats, :] = out

    def back_keys(role):
        pen = penalty(f + offsets[role], f)
        for h in range(2):
            at = slice(h * rows, h * rows + rows)
            st = dot(km[at, :], qs[role], NT)
            pt = jnp.exp(st - (stats[role, h : h + 1, :] + pen))
            dpt = dot(vm[at, :], do[role], NT)
            dst = (pt * (dpt - stats[role, 2 + h : 3 + h, :])).astype(jnp.bfloat16)
            gv = dot(pt.astype(jnp.bfloat16), do[role], NN)
            gk = dot(dst, qs[role], NN)
            if role != OWN:
                gv = gv + gv_acc[at, :]
                gk = gk + gk_acc[at, :]
            gv_acc[at, :] = gv
            gk_acc[at, :] = gk

    loads[0].wait()
    g_all[z] = g_ref[...].T
    loads[1].wait()
    loads[2].wait()
    pl.semaphore_wait(barrier, SPAN - 1 + heads - 1)

    def grad_edge(o):
        src = g_all.at[z, pl.ds(rows - RIM if o == 1 else 0, RIM)]
        return edge(src, mail, 0, o)

    for o in (1, -1):
        grad_edge(o).start()
    hops(g_all, g_s, g_r, range(4))
    for role in FIRST:
        route(kv, kv_s, kv_r, role).start()
    loads[3].wait()
    qs[OWN] = (qs[OWN].astype(jnp.float32) * HEAD_DIM**-0.5).astype(jnp.bfloat16)
    head_columns(qs[OWN].T, qmt)
    loads[4].wait()
    mail[2 * RIM : MAIL - 1, :] = t_ref[...]
    mail[MAIL - 1 : MAIL, :] = jnp.zeros((1, width), jnp.bfloat16)
    loads[5].wait()
    grad_acc[...] = jnp.zeros_like(grad_acc)
    forward(0)

    for o in (1, -1):
        grad_edge(o).wait_recv()
    for i in range(1, heads):
        post(mail, mail_all, m_s, m_r, i).start()
    mail_all[z] = mail[...]
    route(kv, kv_s, kv_r, PAIR).wait_recv()
    forward(1)
    head_rows(kv[OWN, 0], km)
    head_rows(kv[OWN, 1], vm)
    conv_group(z)
    arrive(g_all, g_s, g_r, (0, 1))
    hops(g_all, g_s, g_r, (4, 5, 6, 7))
    route(kv, kv_s, kv_r, UP).wait_recv()
    route(kv, kv_s, kv_r, DOWN).wait_recv()
    for role in SECOND:
        route(kv, kv_s, kv_r, role).start()
    for role in FIRST:
        route(qs, q_s, q_r, role).start()
    forward(2)
    for i in range(1, heads):
        weight(i).start()
    for role in SECOND:
        route(kv, kv_s, kv_r, role).wait_recv()
    forward(3)
    route(kv, kv_s, kv_r, FAR).wait_recv()
    forward(4)

    attended = (acc[...] * by_head(1.0 / total[...])).astype(jnp.bfloat16)
    at_all[z] = attended
    hops(at_all, at_s, at_r, range(4))
    by_frame = attended.T
    ends[0:RIM, :] = by_frame[rows - RIM : rows, :]
    ends[RIM : 2 * RIM, :] = by_frame[0:RIM, :]

    def attended_edge(o):
        return edge(ends.at[pl.ds(0 if o == 1 else RIM, RIM)], rim, 1, o)

    for o in (1, -1):
        attended_edge(o).start()
    logsum = peak[...] + jnp.log(total[...])
    stats[OWN, 0:1, :] = logsum[:, 0:rows]
    stats[OWN, 1:2, :] = logsum[:, rows : 2 * rows]
    stats[OWN, 4:8, :] = jnp.zeros((4, rows), jnp.float32)

    arrive(g_all, g_s, g_r, (2, 3))
    for i in range(1, heads):
        posted(mail, mail_all, m_s, m_r, i).wait_recv()

    def near_groups(i, carry):
        conv_group(zrel(i - 2 + i // 2))
        return carry

    lax.fori_loop(0, 4, near_groups, 0)
    for role in (UP, DOWN):
        route(qs, q_s, q_r, role).wait_recv()
    for role in SECOND:
        route(qs, q_s, q_r, role).start()
    for o in (1, -1):
        attended_edge(o).wait_recv()
    for i in range(1, heads):
        post(rim, rim_all, e_s, e_r, i).start()
    rim_all[z] = rim[...]
    for role in range(SPAN):
        kt[role] = kv[role, 0].T
    arrive(g_all, g_s, g_r, (4, 5, 6, 7))

    def far_groups(i, carry):
        conv_group(zrel(i + 3))
        return carry

    lax.fori_loop(0, 3, far_groups, 0)

    grad_t = grad_acc[...].astype(jnp.bfloat16)
    do[OWN] = grad_t.T
    for role in FIRST:
        route(do, do_s, do_r, role).start()
    product = grad_t.astype(jnp.float32) * at_all[z].astype(jnp.float32)
    stats[OWN, 2:3, :] = jnp.sum(product[0:HEAD_DIM, :], axis=0, keepdims=True)
    stats[OWN, 3:4, :] = jnp.sum(product[HEAD_DIM:width, :], axis=0, keepdims=True)
    for role in range(1, SPAN):
        direct(role).start()
    head_columns(grad_t, dmt)

    arrive(at_all, at_s, at_r, (0, 1))
    hops(at_all, at_s, at_r, (4, 5, 6, 7))
    back_queries(0)
    wcol[z] = w_ref[:, part(z)]
    for i in range(1, heads):
        src = zrel(i)
        remote(w_ref.at[:, part(z)], wcol.at[src], w_s.at[i], w_r.at[src], (f, src)).wait_recv()
    for i in range(heads):
        wcol_t[:, i * width : (i + 1) * width] = wcol[i].T
    back_queries(1)
    dq_ref[...] = acc[...].T.astype(jnp.bfloat16)
    for role in (UP, DOWN):
        route(do, do_s, do_r, role).wait_recv()
    for role in SECOND:
        route(do, do_s, do_r, role).start()
    back_keys(OWN)

    def keys_of(role):
        if role not in (UP, DOWN):
            route(qs, q_s, q_r, role).wait_recv()
            route(do, do_s, do_r, role).wait_recv()
        direct(role).wait_recv()
        back_keys(role)

    keys_of(PAIR)
    keys_of(UP)
    keys_of(DOWN)
    keys_of(PAIR_UP)
    keys_of(PAIR_DOWN)
    keys_of(FAR)
    dv_ref[...] = jnp.where(low, gv_acc[0:rows, :], gv_acc[rows : 2 * rows, :]).astype(jnp.bfloat16)
    dk_ref[...] = jnp.where(low, gk_acc[0:rows, :], gk_acc[rows : 2 * rows, :]).astype(jnp.bfloat16)

    for i in range(1, heads):
        posted(rim, rim_all, e_s, e_r, i).wait_recv()
    arrive(at_all, at_s, at_r, range(2, len(HOPS)))
    side = jnp.zeros((2 * RIM, width), jnp.float32)
    for i in range(heads):
        side = side + dot(rim_all[i], wcol[i], NN)
    side = side.astype(jnp.bfloat16)
    gathered = at_all[...].reshape(heads * width, rows)
    mixed = dot(wcol_t[...], gathered, NN).T.astype(jnp.bfloat16)
    pad[RIM : RIM + rows, :] = mixed.astype(jnp.float32)
    taps[...] = mail_all[z, 2 * RIM : MAIL, :].astype(jnp.float32)
    conv(side[0:RIM, :], side[RIM : 2 * RIM, :], False, conv_tmp)
    co_ref[...] = conv_tmp[...].T

    for o in (1, -1):
        grad_edge(o).wait_send()
        attended_edge(o).wait_send()
    for role in range(1, SPAN):
        route(kv, kv_s, kv_r, role).wait_send()
        route(qs, q_s, q_r, role).wait_send()
        route(do, do_s, do_r, role).wait_send()
        direct(role).wait_send()
    for i in range(1, heads):
        weight(i).wait_send()
        post(mail, mail_all, m_s, m_r, i).wait_send()
        post(rim, rim_all, e_s, e_r, i).wait_send()
    for n in range(len(HOPS)):
        hop(g_all, g_s, g_r, n).wait_send()
        hop(at_all, at_s, at_r, n).wait_send()


def copy_out(*refs):
    half = len(refs) // 2
    sources, targets, sems = refs[:half], refs[half : 2 * half], refs[-1]
    copies = [
        pltpu.make_async_copy(src, dst, sems.at[n]) for n, (src, dst) in enumerate(zip(sources, targets))
    ]
    for copy in copies:
        copy.start()
    for copy in copies:
        copy.wait()


def on_device(queries, keys, values, out_weight, conv_kernel, grad_out, pattern, counts):
    _, rows, width = queries.shape
    frames, heads = lax.axis_size("frame"), lax.axis_size("head")
    bf, f32 = jnp.bfloat16, jnp.float32
    block, tall = (rows, width), (width, rows)
    hbm = pl.BlockSpec(memory_space=pltpu.HBM)
    smem = pl.BlockSpec(memory_space=pltpu.SMEM)
    dma = pltpu.SemaphoreType.DMA
    vmem = pl.BlockSpec(memory_space=pltpu.VMEM)
    shapes = [
        jax.ShapeDtypeStruct(tall, bf),
        jax.ShapeDtypeStruct(block, bf),
        jax.ShapeDtypeStruct(block, bf),
        jax.ShapeDtypeStruct(block, bf),
    ]
    results = pl.pallas_call(
        partial(kernel, frames, heads),
        out_shape=shapes,
        in_specs=[hbm] * 6 + [smem] * 2,
        out_specs=[vmem] * 4,
        scratch_shapes=[
            pltpu.VMEM(out_weight.shape, bf),
            pltpu.VMEM(conv_kernel.shape, bf),
            pltpu.VMEM(tall, bf),
            pltpu.VMEM((SPAN, 2) + block, bf),
            pltpu.VMEM((SPAN,) + tall, bf),
            pltpu.VMEM((SPAN,) + tall, bf),
            pltpu.VMEM((SPAN,) + block, bf),
            pltpu.VMEM((SPAN,) + block, bf),
            pltpu.VMEM((SPAN, 8, rows), f32),
            pltpu.VMEM((heads,) + block, bf),
            pltpu.VMEM((heads,) + tall, bf),
            pltpu.VMEM((MAIL, width), bf),
            pltpu.VMEM((heads, MAIL, width), bf),
            pltpu.VMEM((2 * RIM, width), bf),
            pltpu.VMEM((2 * RIM, width), bf),
            pltpu.VMEM((heads, 2 * RIM, width), bf),
            pltpu.VMEM((heads, width, width), bf),
            pltpu.VMEM((width, heads * width), bf),
            pltpu.VMEM(block, bf),
            pltpu.VMEM((rows + 2 * RIM, width), f32),
            pltpu.VMEM((2 * RIM, width), f32),
            pltpu.VMEM(tall, f32),
            pltpu.VMEM((width, 2 * rows), bf),
            pltpu.VMEM((width, 2 * rows), bf),
            pltpu.VMEM((2 * rows, width), bf),
            pltpu.VMEM((2 * rows, width), bf),
            pltpu.VMEM((SPAN, rows, 2 * rows), bf),
            pltpu.VMEM((len(GROUPS), 1, 2 * rows), f32),
            pltpu.VMEM((1, 2 * rows), f32),
            pltpu.VMEM((1, 2 * rows), f32),
            pltpu.VMEM(tall, f32),
            pltpu.VMEM((2 * rows, width), f32),
            pltpu.VMEM((2 * rows, width), f32),
            dma((6,)),
        ]
        + [dma((SPAN,))] * 8
        + [dma((heads,))] * 10
        + [dma((2, 2))] * 2,
        compiler_params=pltpu.CompilerParams(
            collective_id=0, has_side_effects=True, vmem_limit_bytes=56 * 1024 * 1024
        ),
    )(
        queries.reshape(block),
        keys.reshape(block),
        values.reshape(block),
        out_weight,
        conv_kernel,
        grad_out.reshape(width, rows),
        jnp.transpose(pattern, (2, 0, 1)),
        counts,
    )
    conv_out, dq, dk, dv = pl.pallas_call(
        copy_out,
        out_shape=shapes,
        in_specs=[vmem] * 4,
        out_specs=[hbm] * 4,
        scratch_shapes=[dma((4,))],
    )(*results)
    return (
        conv_out.reshape(grad_out.shape),
        dq.reshape(queries.shape),
        dk.reshape(keys.shape),
        dv.reshape(values.shape),
    )


def solution(mesh):
    return jax.shard_map(
        on_device,
        mesh=mesh,
        in_specs=(
            P(None, "frame", "head"),
            P(None, "frame", "head"),
            P(None, "frame", "head"),
            P("head", None),
            P(None, "head"),
            P("head", None, "frame"),
            P(),
            P(),
        ),
        out_specs=(
            P("head", None, "frame"),
            P(None, "frame", "head"),
            P(None, "frame", "head"),
            P(None, "frame", "head"),
        ),
        check_vma=False,
    )
```

```python
from functools import partial, reduce

import jax
import jax.numpy as jnp
from jax import lax
from jax.experimental import pallas as pl
from jax.experimental.pallas import tpu as pltpu
from jax.sharding import PartitionSpec as P

HEAD_DIM = 64
KERNEL = 31
SPAN = 7
HUGE = 1e30
MESH = pl.DeviceIdType.MESH
RIM = 16
MAIL = 64
QUARTERS = 4

NT = (((1,), (1,)), ((), ()))
NN = (((1,), (0,)), ((), ()))

OWN, PAIR, UP, DOWN, PAIR_UP, PAIR_DOWN, FAR = range(SPAN)
GROUPS = ((OWN,), (PAIR,), (UP, DOWN), (PAIR_UP, PAIR_DOWN), (FAR,))


def dot(a, b, dims):
    return lax.dot_general(a, b, dims, preferred_element_type=jnp.float32)


def remote(src, dst, s, r, dev):
    return pltpu.make_async_remote_copy(
        src_ref=src, dst_ref=dst, send_sem=s, recv_sem=r, device_id=dev, device_id_type=MESH
    )


def kernel(
    frames,
    heads,
    q_hbm,
    k_hbm,
    v_hbm,
    w_hbm,
    t_hbm,
    g_hbm,
    pat_ref,
    cnt_ref,
    co_hbm,
    dq_hbm,
    dk_hbm,
    dv_hbm,
    co_ref,
    dq_ref,
    dk_ref,
    dv_ref,
    w_ref,
    t_ref,
    g_ref,
    kv,
    kt,
    vt,
    qs,
    do,
    stats,
    g_all,
    at_all,
    mail,
    mail_all,
    ends,
    rim,
    rim_all,
    side_ref,
    wcol,
    wcol_t,
    conv_tmp,
    pad,
    taps,
    grad_acc,
    qmt,
    dmt,
    km,
    vm,
    probs,
    key_probs,
    peaks,
    peak,
    total,
    acc,
    gk_acc,
    gv_acc,
    in_s,
    out_s,
    kv_s,
    kv_r,
    q_s,
    q_r,
    do_s,
    do_r,
    st_s,
    st_r,
    w_s,
    w_r,
    x_s,
    x_r,
    g_s,
    g_r,
    at_s,
    at_r,
    m_s,
    m_r,
    e_s,
    e_r,
    h_s,
    h_r,
):
    f = lax.axis_index("frame")
    z = lax.axis_index("head")
    rows, width = kv.shape[2], kv.shape[3]
    odd = lax.rem(f, 2)
    sign = 2 * odd - 1

    def fdev(o):
        return (lax.rem(f + o + frames, frames), z)

    def zrel(i):
        return lax.rem(z + i + heads, heads)

    def part(index, size=width, start=0):
        return pl.ds(pl.multiple_of(index * width + start, size), size)

    offsets = (0, -sign, 2, -2, 2 - sign, -2 - sign, 3 * sign)

    loads = [
        pltpu.make_async_copy(src, dst, in_s.at[n])
        for n, (src, dst) in enumerate(
            (
                (g_hbm, g_ref),
                (k_hbm, kv.at[OWN, 0]),
                (v_hbm, kv.at[OWN, 1]),
                (q_hbm, qs.at[OWN]),
                (t_hbm, t_ref),
                (w_hbm, w_ref),
            )
        )
    ]
    for load in loads:
        load.start()

    barrier = pltpu.get_barrier_semaphore()
    for o in offsets[1:]:
        pl.semaphore_signal(barrier, inc=1, device_id=fdev(o), device_id_type=MESH)
    for i in range(1, heads):
        pl.semaphore_signal(barrier, inc=1, device_id=(f, zrel(i)), device_id_type=MESH)
    for d in range(1, QUARTERS):
        pl.semaphore_signal(barrier, inc=1, device_id=fdev(d * (frames // QUARTERS)), device_id_type=MESH)

    def route(buf, s, r, role):
        src, o = {
            PAIR: (OWN, -sign),
            DOWN: (OWN, 2),
            UP: (OWN, -2),
            FAR: (UP + odd, sign) if buf is kv else (OWN, 3 * sign),
            PAIR_UP: (UP, -sign),
            PAIR_DOWN: (DOWN, -sign),
        }[role]
        return remote(buf.at[src], buf.at[role], s.at[role], r.at[role], fdev(o))

    FIRST, SECOND = (UP, DOWN, PAIR, FAR), (PAIR_UP, PAIR_DOWN)

    def direct(role, which):
        o = {
            PAIR: -sign,
            DOWN: 2,
            UP: -2,
            PAIR_DOWN: 2 - sign,
            PAIR_UP: -2 - sign,
            FAR: 3 * sign,
        }[role]
        at = pl.ds(8 * which, 8)
        return remote(
            stats.at[OWN, at], stats.at[role, at], st_s.at[which, role], st_r.at[which, role], fdev(o)
        )

    def edge(src, dst, which, o):
        side = 0 if o == 1 else 1
        at = pl.ds(side * RIM, RIM)
        return remote(src, dst.at[at], h_s.at[which, side], h_r.at[which, side], fdev(o))

    def post(src, dst, s, r, i):
        return remote(src, dst.at[z], s.at[i], r.at[z], (f, zrel(i)))

    def posted(src, dst, s, r, i):
        origin = zrel(i)
        return remote(src, dst.at[origin], s.at[i], r.at[origin], (f, origin))

    stride, share = frames // QUARTERS, width // QUARTERS
    own_rows = pl.ds(pl.multiple_of((f // stride) * share, share), share)

    def weight(i, arrived=False):
        there = zrel(i)
        if arrived:
            return remote(wcol.at[there, own_rows], wcol.at[there, own_rows], w_s.at[i], w_r.at[there], (f, there))
        return remote(w_ref.at[own_rows, part(there)], wcol.at[z, own_rows], w_s.at[i], w_r.at[z], (f, there))

    def quarter(d, arrived=False):
        back = lax.rem(f // stride + QUARTERS - d, QUARTERS) if arrived else f // stride
        at = pl.ds(pl.multiple_of(back * share, share), share)
        return remote(wcol.at[:, at], wcol.at[:, at], x_s.at[d], x_r.at[d], fdev(d * stride))

    HOPS = ((0, 2), (0, -2), (0, 1), (0, -1), (-2, 1), (2, -1), (-2, 2), (2, -2))

    def hop(buf, s, r, n, arrived=False):
        origin, target = HOPS[n]
        slot = zrel(origin - target if arrived else origin)
        block = buf.at[slot]
        if n >= 6:
            half = buf.shape[1] // 2
            block = buf.at[slot, pl.ds(half * (n - 6), half)]
        return remote(block, block, s.at[n], r.at[n], (f, zrel(target)))

    def hops(buf, s, r, which):
        for n in which:
            hop(buf, s, r, n).start()

    def arrive(buf, s, r, which):
        for n in which:
            hop(buf, s, r, n, True).wait_recv()

    def penalty(query_block, key_block):
        inside = (query_block >= 0) & (query_block < frames) & (key_block >= 0) & (key_block < frames)
        safe = lax.rem(query_block + frames, frames)
        number = cnt_ref[0, safe]
        hit = False
        for entry in range(pat_ref.shape[0]):
            hit = hit | ((pat_ref[entry, 0, safe] == key_block) & (entry < number))
        return jnp.where(inside & hit, 0.0, HUGE)

    def conv(left, right, flip, out):
        pad[0:RIM, :] = jnp.where(f > 0, left.astype(jnp.float32), 0.0)
        pad[RIM + rows : 2 * RIM + rows, :] = jnp.where(f < frames - 1, right.astype(jnp.float32), 0.0)
        step = 64
        for c in range(rows // step):
            total_c = jnp.zeros((step, width), jnp.float32)
            for t in range(KERNEL):
                tap = KERNEL - 1 - t if flip else t
                total_c = total_c + taps[tap : tap + 1, :] * pad[c * step + t + 1 : c * step + t + 1 + step, :]
            out[c * step : c * step + step, :] = total_c.astype(jnp.bfloat16)

    def conv_group(group):
        pad[RIM : RIM + rows, :] = g_all[group].astype(jnp.float32)
        taps[...] = mail_all[group, 2 * RIM : MAIL, :].astype(jnp.float32)
        conv(mail_all[group, 0:RIM, :], mail_all[group, RIM : 2 * RIM, :], True, conv_tmp)
        grad_acc[...] += dot(w_ref[:, part(group)], conv_tmp[...], NT)

    def head_columns(x, dst):
        dst[0:HEAD_DIM, 0:rows] = x[0:HEAD_DIM, :]
        dst[HEAD_DIM:width, rows : 2 * rows] = x[HEAD_DIM:width, :]
        dst[0:HEAD_DIM, rows : 2 * rows] = jnp.zeros((HEAD_DIM, rows), jnp.bfloat16)
        dst[HEAD_DIM:width, 0:rows] = jnp.zeros((HEAD_DIM, rows), jnp.bfloat16)

    low = lax.broadcasted_iota(jnp.int32, (rows, width), 1) < HEAD_DIM

    def head_rows(x, dst):
        x = x.astype(jnp.float32)
        dst[0:rows, :] = jnp.where(low, x, 0.0).astype(jnp.bfloat16)
        dst[rows : 2 * rows, :] = jnp.where(low, 0.0, x).astype(jnp.bfloat16)

    def by_head(row):
        return jnp.concatenate(
            [
                jnp.broadcast_to(row[:, 0:rows], (HEAD_DIM, rows)),
                jnp.broadcast_to(row[:, rows : 2 * rows], (HEAD_DIM, rows)),
            ],
            axis=0,
        )

    def forward(group):
        roles = GROUPS[group]
        for role in roles:
            vt[role] = kv[role, 1].T
        scores = [dot(kv[role, 0], qmt[...], NN) for role in roles]
        pens = [penalty(f, f + offsets[role]) for role in roles]
        m = reduce(
            jnp.maximum, [jnp.max(s, axis=0, keepdims=True) - pen for s, pen in zip(scores, pens)]
        )
        if group > 0:
            old = peak[...]
            m = jnp.maximum(old, m)
        sums, outs = [], []
        for role, s, pen in zip(roles, scores, pens):
            p = jnp.exp(s - (m + pen))
            sums.append(jnp.sum(p, axis=0, keepdims=True))
            weights = p.astype(jnp.bfloat16)
            probs[role] = weights
            outs.append(
                jnp.concatenate(
                    [
                        dot(vt[role, 0:HEAD_DIM, :], weights[:, 0:rows], NN),
                        dot(vt[role, HEAD_DIM:width, :], weights[:, rows : 2 * rows], NN),
                    ],
                    axis=0,
                )
            )
        row_sum, out = reduce(jnp.add, sums), reduce(jnp.add, outs)
        if group > 0:
            fade = jnp.exp(old - m)
            row_sum = row_sum + total[...] * fade
            out = out + acc[...] * by_head(fade)
        peak[...] = m
        peaks[group] = m
        total[...] = row_sum
        acc[...] = out

    def back_queries(h):
        cols = slice(h * rows, h * rows + rows)
        feats = slice(h * HEAD_DIM, (h + 1) * HEAD_DIM)
        out = jnp.zeros((HEAD_DIM, rows), jnp.float32)
        factor = HEAD_DIM**-0.5 / total[:, cols]
        delta = stats[OWN, 8 + h : 9 + h, :]
        for group, roles in enumerate(GROUPS):
            scale = factor * jnp.exp(peaks[group, :, cols] - peak[:, cols])
            for role in roles:
                dp = dot(kv[role, 1], dmt[:, cols], NN)
                ds = (probs[role, :, cols].astype(jnp.float32) * (dp - delta)).astype(jnp.bfloat16)
                out = out + scale * dot(kt[role, feats, :], ds, NN)
        acc[feats, :] = out

    def key_weights(role):
        pen = penalty(f + offsets[role], f)
        for h in range(2):
            at = slice(h * rows, h * rows + rows)
            st = dot(km[at, :], qs[role], NT)
            key_probs[role, at, :] = jnp.exp(st - (stats[role, h : h + 1, :] + pen)).astype(jnp.bfloat16)

    def back_keys(role):
        for h in range(2):
            at = slice(h * rows, h * rows + rows)
            pt = key_probs[role, at, :]
            dpt = dot(vm[at, :], do[role], NT)
            dst = (pt.astype(jnp.float32) * (dpt - stats[role, 8 + h : 9 + h, :])).astype(jnp.bfloat16)
            gv = dot(pt, do[role], NN)
            gk = dot(dst, qs[role], NN)
            if role != OWN:
                gv = gv + gv_acc[at, :]
                gk = gk + gk_acc[at, :]
            gv_acc[at, :] = gv
            gk_acc[at, :] = gk

    loads[0].wait()
    g_all[z] = g_ref[...].T
    loads[1].wait()
    loads[2].wait()
    pl.semaphore_wait(barrier, SPAN - 1 + heads - 1 + QUARTERS - 1)

    def grad_edge(o):
        src = g_all.at[z, pl.ds(rows - RIM if o == 1 else 0, RIM)]
        return edge(src, mail, 0, o)

    for o in (1, -1):
        grad_edge(o).start()
    hops(g_all, g_s, g_r, (0, 1))
    for role in (UP, DOWN, PAIR):
        route(kv, kv_s, kv_r, role).start()
    loads[3].wait()
    qs[OWN] = (qs[OWN].astype(jnp.float32) * HEAD_DIM**-0.5).astype(jnp.bfloat16)
    head_columns(qs[OWN].T, qmt)
    loads[4].wait()
    mail[2 * RIM : MAIL - 1, :] = t_ref[...]
    mail[MAIL - 1 : MAIL, :] = jnp.zeros((1, width), jnp.bfloat16)
    loads[5].wait()
    for i in range(1, heads):
        weight(i).start()
    wcol[z, own_rows] = w_ref[own_rows, part(z)]
    grad_acc[...] = jnp.zeros_like(grad_acc)
    forward(0)

    for o in (1, -1):
        grad_edge(o).wait_recv()
    for i in range(1, heads):
        post(mail, mail_all, m_s, m_r, i).start()
    mail_all[z] = mail[...]
    route(kv, kv_s, kv_r, PAIR).wait_recv()
    hops(g_all, g_s, g_r, (2, 3))
    forward(1)
    head_rows(kv[OWN, 0], km)
    head_rows(kv[OWN, 1], vm)
    conv_group(z)
    arrive(g_all, g_s, g_r, (0, 1))
    hops(g_all, g_s, g_r, (4, 5, 6, 7))
    route(kv, kv_s, kv_r, UP).wait_recv()
    route(kv, kv_s, kv_r, DOWN).wait_recv()
    for role in (FAR,) + SECOND:
        route(kv, kv_s, kv_r, role).start()
    for role in FIRST:
        route(qs, q_s, q_r, role).start()
    forward(2)
    for i in range(1, heads):
        weight(i, True).wait_recv()
    for d in range(1, QUARTERS):
        quarter(d).start()
    for role in SECOND:
        route(kv, kv_s, kv_r, role).wait_recv()
    forward(3)
    route(kv, kv_s, kv_r, FAR).wait_recv()
    forward(4)

    attended = (acc[...] * by_head(1.0 / total[...])).astype(jnp.bfloat16)
    at_all[z] = attended
    hops(at_all, at_s, at_r, (0, 1))
    by_frame = attended.T
    ends[0:RIM, :] = by_frame[rows - RIM : rows, :]
    ends[RIM : 2 * RIM, :] = by_frame[0:RIM, :]

    def attended_edge(o):
        return edge(ends.at[pl.ds(0 if o == 1 else RIM, RIM)], rim, 1, o)

    for o in (1, -1):
        attended_edge(o).start()
    logsum = peak[...] + jnp.log(total[...])
    stats[OWN, 0:1, :] = logsum[:, 0:rows]
    stats[OWN, 1:2, :] = logsum[:, rows : 2 * rows]
    stats[OWN, 2:8, :] = jnp.zeros((6, rows), jnp.float32)
    for role in range(1, SPAN):
        direct(role, 0).start()

    arrive(g_all, g_s, g_r, (2, 3))
    for i in range(1, heads):
        posted(mail, mail_all, m_s, m_r, i).wait_recv()

    def near_groups(i, carry):
        conv_group(zrel(i - 2 + i // 2))
        return carry

    lax.fori_loop(0, 4, near_groups, 0)
    hops(at_all, at_s, at_r, (2, 3))
    for role in (UP, DOWN):
        route(qs, q_s, q_r, role).wait_recv()
    for role in SECOND:
        route(qs, q_s, q_r, role).start()
    key_weights(OWN)
    for role in range(SPAN):
        kt[role] = kv[role, 0].T
    for d in range(1, QUARTERS):
        quarter(d, True).wait_recv()
    for i in range(heads):
        wcol_t[:, i * width : (i + 1) * width] = wcol[i].T
    arrive(g_all, g_s, g_r, (4, 5, 6, 7))

    def far_groups(i, carry):
        conv_group(zrel(i + 3))
        return carry

    lax.fori_loop(0, 3, far_groups, 0)

    grad_t = grad_acc[...].astype(jnp.bfloat16)
    do[OWN] = grad_t.T
    for role in FIRST:
        route(do, do_s, do_r, role).start()
    product = grad_t.astype(jnp.float32) * at_all[z].astype(jnp.float32)
    stats[OWN, 8:9, :] = jnp.sum(product[0:HEAD_DIM, :], axis=0, keepdims=True)
    stats[OWN, 9:10, :] = jnp.sum(product[HEAD_DIM:width, :], axis=0, keepdims=True)
    stats[OWN, 10:16, :] = jnp.zeros((6, rows), jnp.float32)
    for role in range(1, SPAN):
        direct(role, 1).start()
    head_columns(grad_t, dmt)

    def ready(role):
        if role not in (OWN, UP, DOWN):
            route(qs, q_s, q_r, role).wait_recv()
        if role != OWN:
            direct(role, 0).wait_recv()
        key_weights(role)

    back_queries(0)
    for o in (1, -1):
        attended_edge(o).wait_recv()
    for i in range(1, heads):
        post(rim, rim_all, e_s, e_r, i).start()
    rim_all[z] = rim[...]
    back_queries(1)
    dq_ref[...] = acc[...].T.astype(jnp.bfloat16)
    stores = [
        pltpu.make_async_copy(src, dst, out_s.at[n])
        for n, (src, dst) in enumerate(
            ((dq_ref, dq_hbm), (dk_ref, dk_hbm), (dv_ref, dv_hbm), (co_ref, co_hbm))
        )
    ]
    stores[0].start()
    ready(PAIR)
    arrive(at_all, at_s, at_r, (0, 1))
    hops(at_all, at_s, at_r, (4, 5, 6, 7))
    ready(UP)
    ready(DOWN)
    for role in (UP, DOWN):
        route(do, do_s, do_r, role).wait_recv()
    for role in SECOND:
        route(do, do_s, do_r, role).start()
    ready(PAIR_UP)
    ready(PAIR_DOWN)
    ready(FAR)
    back_keys(OWN)
    for i in range(1, heads):
        posted(rim, rim_all, e_s, e_r, i).wait_recv()
    side = jnp.zeros((2 * RIM, width), jnp.float32)
    for i in range(heads):
        side = side + dot(rim_all[i], wcol[i], NN)
    side_ref[...] = side.astype(jnp.bfloat16)
    taps[...] = mail_all[z, 2 * RIM : MAIL, :].astype(jnp.float32)

    def keys_of(role):
        if role not in (UP, DOWN):
            route(do, do_s, do_r, role).wait_recv()
        direct(role, 1).wait_recv()
        back_keys(role)

    keys_of(PAIR)
    keys_of(UP)
    keys_of(DOWN)
    keys_of(PAIR_UP)
    keys_of(PAIR_DOWN)
    keys_of(FAR)
    dv_ref[...] = jnp.where(low, gv_acc[0:rows, :], gv_acc[rows : 2 * rows, :]).astype(jnp.bfloat16)
    dk_ref[...] = jnp.where(low, gk_acc[0:rows, :], gk_acc[rows : 2 * rows, :]).astype(jnp.bfloat16)
    stores[1].start()
    stores[2].start()

    arrive(at_all, at_s, at_r, range(2, len(HOPS)))
    gathered = at_all[...].reshape(heads * width, rows)
    mixed = dot(wcol_t[...], gathered, NN).T.astype(jnp.bfloat16)
    pad[RIM : RIM + rows, :] = mixed.astype(jnp.float32)
    conv(side_ref[0:RIM, :], side_ref[RIM : 2 * RIM, :], False, conv_tmp)
    co_ref[...] = conv_tmp[...].T
    stores[3].start()

    for o in (1, -1):
        grad_edge(o).wait_send()
        attended_edge(o).wait_send()
    for role in range(1, SPAN):
        route(kv, kv_s, kv_r, role).wait_send()
        route(qs, q_s, q_r, role).wait_send()
        route(do, do_s, do_r, role).wait_send()
        direct(role, 0).wait_send()
        direct(role, 1).wait_send()
    for i in range(1, heads):
        weight(i).wait_send()
        post(mail, mail_all, m_s, m_r, i).wait_send()
        post(rim, rim_all, e_s, e_r, i).wait_send()
    for d in range(1, QUARTERS):
        quarter(d).wait_send()
    for n in range(len(HOPS)):
        hop(g_all, g_s, g_r, n).wait_send()
        hop(at_all, at_s, at_r, n).wait_send()
    for store in stores:
        store.wait()


def copy_out(*refs):
    half = len(refs) // 2
    sources, targets, sems = refs[:half], refs[half : 2 * half], refs[-1]
    copies = [
        pltpu.make_async_copy(src, dst, sems.at[n]) for n, (src, dst) in enumerate(zip(sources, targets))
    ]
    for copy in copies:
        copy.start()
    for copy in copies:
        copy.wait()


def on_device(queries, keys, values, out_weight, conv_kernel, grad_out, pattern, counts):
    _, rows, width = queries.shape
    frames, heads = lax.axis_size("frame"), lax.axis_size("head")
    bf, f32 = jnp.bfloat16, jnp.float32
    block, tall = (rows, width), (width, rows)
    hbm = pl.BlockSpec(memory_space=pltpu.HBM)
    smem = pl.BlockSpec(memory_space=pltpu.SMEM)
    dma = pltpu.SemaphoreType.DMA
    vmem = pl.BlockSpec(memory_space=pltpu.VMEM)
    shapes = [
        jax.ShapeDtypeStruct(tall, bf),
        jax.ShapeDtypeStruct(block, bf),
        jax.ShapeDtypeStruct(block, bf),
        jax.ShapeDtypeStruct(block, bf),
    ]
    results = pl.pallas_call(
        partial(kernel, frames, heads),
        out_shape=shapes,
        in_specs=[hbm] * 6 + [smem] * 2,
        out_specs=[hbm] * 4,
        scratch_shapes=[
            pltpu.VMEM(tall, bf),
            pltpu.VMEM(block, bf),
            pltpu.VMEM(block, bf),
            pltpu.VMEM(block, bf),
            pltpu.VMEM(out_weight.shape, bf),
            pltpu.VMEM(conv_kernel.shape, bf),
            pltpu.VMEM(tall, bf),
            pltpu.VMEM((SPAN, 2) + block, bf),
            pltpu.VMEM((SPAN,) + tall, bf),
            pltpu.VMEM((SPAN,) + tall, bf),
            pltpu.VMEM((SPAN,) + block, bf),
            pltpu.VMEM((SPAN,) + block, bf),
            pltpu.VMEM((SPAN, 16, rows), f32),
            pltpu.VMEM((heads,) + block, bf),
            pltpu.VMEM((heads,) + tall, bf),
            pltpu.VMEM((MAIL, width), bf),
            pltpu.VMEM((heads, MAIL, width), bf),
            pltpu.VMEM((2 * RIM, width), bf),
            pltpu.VMEM((2 * RIM, width), bf),
            pltpu.VMEM((heads, 2 * RIM, width), bf),
            pltpu.VMEM((2 * RIM, width), bf),
            pltpu.VMEM((heads, width, width), bf),
            pltpu.VMEM((width, heads * width), bf),
            pltpu.VMEM(block, bf),
            pltpu.VMEM((rows + 2 * RIM, width), f32),
            pltpu.VMEM((2 * RIM, width), f32),
            pltpu.VMEM(tall, f32),
            pltpu.VMEM((width, 2 * rows), bf),
            pltpu.VMEM((width, 2 * rows), bf),
            pltpu.VMEM((2 * rows, width), bf),
            pltpu.VMEM((2 * rows, width), bf),
            pltpu.VMEM((SPAN, rows, 2 * rows), bf),
            pltpu.VMEM((SPAN, 2 * rows, rows), bf),
            pltpu.VMEM((len(GROUPS), 1, 2 * rows), f32),
            pltpu.VMEM((1, 2 * rows), f32),
            pltpu.VMEM((1, 2 * rows), f32),
            pltpu.VMEM(tall, f32),
            pltpu.VMEM((2 * rows, width), f32),
            pltpu.VMEM((2 * rows, width), f32),
            dma((6,)),
            dma((4,)),
        ]
        + [dma((SPAN,))] * 6
        + [dma((2, SPAN))] * 2
        + [dma((heads,))] * 2
        + [dma((QUARTERS,))] * 2
        + [dma((heads,))] * 8
        + [dma((2, 2))] * 2,
        compiler_params=pltpu.CompilerParams(
            collective_id=0, has_side_effects=True, vmem_limit_bytes=56 * 1024 * 1024
        ),
    )(
        queries.reshape(block),
        keys.reshape(block),
        values.reshape(block),
        out_weight,
        conv_kernel,
        grad_out.reshape(width, rows),
        jnp.transpose(pattern, (2, 0, 1)),
        counts,
    )
    conv_out, dq, dk, dv = pl.pallas_call(
        copy_out,
        out_shape=shapes,
        in_specs=[vmem] * 4,
        out_specs=[hbm] * 4,
        scratch_shapes=[dma((4,))],
    )(*results)
    return (
        conv_out.reshape(grad_out.shape),
        dq.reshape(queries.shape),
        dk.reshape(keys.shape),
        dv.reshape(values.shape),
    )


def solution(mesh):
    return jax.shard_map(
        on_device,
        mesh=mesh,
        in_specs=(
            P(None, "frame", "head"),
            P(None, "frame", "head"),
            P(None, "frame", "head"),
            P("head", None),
            P(None, "head"),
            P("head", None, "frame"),
            P(),
            P(),
        ),
        out_specs=(
            P("head", None, "frame"),
            P(None, "frame", "head"),
            P(None, "frame", "head"),
            P(None, "frame", "head"),
        ),
        check_vma=False,
    )
```

```python
from functools import partial, reduce

import jax
import jax.numpy as jnp
from jax import lax
from jax.experimental import pallas as pl
from jax.experimental.pallas import tpu as pltpu
from jax.sharding import PartitionSpec as P

HEAD_DIM = 64
KERNEL = 31
SPAN = 7
HUGE = 1e30
MESH = pl.DeviceIdType.MESH
RIM = 16
MAIL = 64
QUARTERS = 4

NT = (((1,), (1,)), ((), ()))
NN = (((1,), (0,)), ((), ()))

OWN, PAIR, UP, DOWN, PAIR_UP, PAIR_DOWN, FAR = range(SPAN)
GROUPS = ((OWN,), (PAIR,), (UP, DOWN), (PAIR_UP, PAIR_DOWN), (FAR,))


def dot(a, b, dims):
    return lax.dot_general(a, b, dims, preferred_element_type=jnp.float32)


def remote(src, dst, s, r, dev):
    return pltpu.make_async_remote_copy(
        src_ref=src, dst_ref=dst, send_sem=s, recv_sem=r, device_id=dev, device_id_type=MESH
    )


def kernel(
    frames,
    heads,
    q_hbm,
    k_hbm,
    v_hbm,
    w_hbm,
    t_hbm,
    g_hbm,
    pat_hbm,
    cnt_hbm,
    co_hbm,
    dq_hbm,
    dk_hbm,
    dv_hbm,
    co_ref,
    dq_ref,
    dk_ref,
    dv_ref,
    w_ref,
    t_ref,
    g_ref,
    pat_ref,
    cnt_ref,
    kv,
    kt,
    vt,
    qs,
    do,
    stats,
    g_all,
    at_all,
    mail,
    mail_all,
    ends,
    rim,
    rim_all,
    side_ref,
    wcol,
    wcol_t,
    conv_tmp,
    pad,
    taps,
    grad_acc,
    qmt,
    dmt,
    km,
    vm,
    probs,
    key_probs,
    peaks,
    peak,
    total,
    acc,
    gk_acc,
    gv_acc,
    in_s,
    out_s,
    kv_s,
    kv_r,
    q_s,
    q_r,
    do_s,
    do_r,
    st_s,
    st_r,
    w_s,
    w_r,
    x_s,
    x_r,
    g_s,
    g_r,
    at_s,
    at_r,
    m_s,
    m_r,
    e_s,
    e_r,
    h_s,
    h_r,
):
    f = lax.axis_index("frame")
    z = lax.axis_index("head")
    rows, width = kv.shape[2], kv.shape[3]
    odd = lax.rem(f, 2)
    sign = 2 * odd - 1

    def fdev(o):
        return (lax.rem(f + o + frames, frames), z)

    def zrel(i):
        return lax.rem(z + i + heads, heads)

    def part(index, size=width, start=0):
        return pl.ds(pl.multiple_of(index * width + start, size), size)

    offsets = (0, -sign, 2, -2, 2 - sign, -2 - sign, 3 * sign)

    barrier = pltpu.get_barrier_semaphore()
    for o in offsets[1:]:
        pl.semaphore_signal(barrier, inc=1, device_id=fdev(o), device_id_type=MESH)
    for i in range(1, heads):
        pl.semaphore_signal(barrier, inc=1, device_id=(f, zrel(i)), device_id_type=MESH)
    for d in range(1, QUARTERS):
        pl.semaphore_signal(barrier, inc=1, device_id=fdev(d * (frames // QUARTERS)), device_id_type=MESH)

    loads = [
        pltpu.make_async_copy(src, dst, in_s.at[n])
        for n, (src, dst) in enumerate(
            (
                (g_hbm, g_ref),
                (k_hbm, kv.at[OWN, 0]),
                (v_hbm, kv.at[OWN, 1]),
                (q_hbm, qs.at[OWN]),
                (t_hbm, t_ref),
                (w_hbm, w_ref),
                (pat_hbm, pat_ref),
                (cnt_hbm, cnt_ref),
            )
        )
    ]
    for load in loads:
        load.start()

    def route(buf, s, r, role):
        src, o = {
            PAIR: (OWN, -sign),
            DOWN: (OWN, 2),
            UP: (OWN, -2),
            FAR: (UP + odd, sign) if buf is kv else (OWN, 3 * sign),
            PAIR_UP: (UP, -sign),
            PAIR_DOWN: (DOWN, -sign),
        }[role]
        return remote(buf.at[src], buf.at[role], s.at[role], r.at[role], fdev(o))

    FIRST, SECOND = (UP, DOWN, PAIR, FAR), (PAIR_UP, PAIR_DOWN)

    def direct(role, which):
        o = {
            PAIR: -sign,
            DOWN: 2,
            UP: -2,
            PAIR_DOWN: 2 - sign,
            PAIR_UP: -2 - sign,
            FAR: 3 * sign,
        }[role]
        at = pl.ds(8 * which, 8)
        return remote(
            stats.at[OWN, at], stats.at[role, at], st_s.at[which, role], st_r.at[which, role], fdev(o)
        )

    def edge(src, dst, which, o):
        side = 0 if o == 1 else 1
        at = pl.ds(side * RIM, RIM)
        return remote(src, dst.at[at], h_s.at[which, side], h_r.at[which, side], fdev(o))

    def post(src, dst, s, r, i):
        return remote(src, dst.at[z], s.at[i], r.at[z], (f, zrel(i)))

    def posted(src, dst, s, r, i):
        origin = zrel(i)
        return remote(src, dst.at[origin], s.at[i], r.at[origin], (f, origin))

    stride, share = frames // QUARTERS, width // QUARTERS
    own_rows = pl.ds(pl.multiple_of((f // stride) * share, share), share)

    def weight(i, arrived=False):
        there = zrel(i)
        if arrived:
            return remote(wcol.at[there, own_rows], wcol.at[there, own_rows], w_s.at[i], w_r.at[there], (f, there))
        return remote(w_ref.at[own_rows, part(there)], wcol.at[z, own_rows], w_s.at[i], w_r.at[z], (f, there))

    def quarter(d, arrived=False):
        back = lax.rem(f // stride + QUARTERS - d, QUARTERS) if arrived else f // stride
        at = pl.ds(pl.multiple_of(back * share, share), share)
        return remote(wcol.at[:, at], wcol.at[:, at], x_s.at[d], x_r.at[d], fdev(d * stride))

    HOPS = ((0, 2), (0, -2), (0, 1), (0, -1), (-2, 1), (2, -1), (-2, 2), (2, -2))

    def hop(buf, s, r, n, arrived=False):
        origin, target = HOPS[n]
        slot = zrel(origin - target if arrived else origin)
        block = buf.at[slot]
        if n >= 6:
            half = buf.shape[1] // 2
            block = buf.at[slot, pl.ds(half * (n - 6), half)]
        return remote(block, block, s.at[n], r.at[n], (f, zrel(target)))

    def hops(buf, s, r, which):
        for n in which:
            hop(buf, s, r, n).start()

    def arrive(buf, s, r, which):
        for n in which:
            hop(buf, s, r, n, True).wait_recv()

    def penalty(query_block, key_block):
        inside = (query_block >= 0) & (query_block < frames) & (key_block >= 0) & (key_block < frames)
        safe = lax.rem(query_block + frames, frames)
        number = cnt_ref[0, safe]
        hit = False
        for entry in range(pat_ref.shape[0]):
            hit = hit | ((pat_ref[entry, 0, safe] == key_block) & (entry < number))
        return jnp.where(inside & hit, 0.0, HUGE)

    def conv(left, right, flip, out):
        pad[0:RIM, :] = jnp.where(f > 0, left.astype(jnp.float32), 0.0)
        pad[RIM + rows : 2 * RIM + rows, :] = jnp.where(f < frames - 1, right.astype(jnp.float32), 0.0)
        step = 64
        for c in range(rows // step):
            total_c = jnp.zeros((step, width), jnp.float32)
            for t in range(KERNEL):
                tap = KERNEL - 1 - t if flip else t
                total_c = total_c + taps[tap : tap + 1, :] * pad[c * step + t + 1 : c * step + t + 1 + step, :]
            out[c * step : c * step + step, :] = total_c.astype(jnp.bfloat16)

    def conv_group(group):
        pad[RIM : RIM + rows, :] = g_all[group].astype(jnp.float32)
        taps[...] = mail_all[group, 2 * RIM : MAIL, :].astype(jnp.float32)
        conv(mail_all[group, 0:RIM, :], mail_all[group, RIM : 2 * RIM, :], True, conv_tmp)
        grad_acc[...] += dot(w_ref[:, part(group)], conv_tmp[...], NT)

    def head_columns(x, dst):
        dst[0:HEAD_DIM, 0:rows] = x[0:HEAD_DIM, :]
        dst[HEAD_DIM:width, rows : 2 * rows] = x[HEAD_DIM:width, :]
        dst[0:HEAD_DIM, rows : 2 * rows] = jnp.zeros((HEAD_DIM, rows), jnp.bfloat16)
        dst[HEAD_DIM:width, 0:rows] = jnp.zeros((HEAD_DIM, rows), jnp.bfloat16)

    low = lax.broadcasted_iota(jnp.int32, (rows, width), 1) < HEAD_DIM

    def head_rows(x, dst):
        x = x.astype(jnp.float32)
        dst[0:rows, :] = jnp.where(low, x, 0.0).astype(jnp.bfloat16)
        dst[rows : 2 * rows, :] = jnp.where(low, 0.0, x).astype(jnp.bfloat16)

    def by_head(row):
        return jnp.concatenate(
            [
                jnp.broadcast_to(row[:, 0:rows], (HEAD_DIM, rows)),
                jnp.broadcast_to(row[:, rows : 2 * rows], (HEAD_DIM, rows)),
            ],
            axis=0,
        )

    def forward(group):
        roles = GROUPS[group]
        for role in roles:
            vt[role] = kv[role, 1].T
        scores = [dot(kv[role, 0], qmt[...], NN) for role in roles]
        pens = [penalty(f, f + offsets[role]) for role in roles]
        m = reduce(
            jnp.maximum, [jnp.max(s, axis=0, keepdims=True) - pen for s, pen in zip(scores, pens)]
        )
        if group > 0:
            old = peak[...]
            m = jnp.maximum(old, m)
        sums, outs = [], []
        for role, s, pen in zip(roles, scores, pens):
            p = jnp.exp(s - (m + pen))
            sums.append(jnp.sum(p, axis=0, keepdims=True))
            weights = p.astype(jnp.bfloat16)
            probs[role] = weights
            outs.append(
                jnp.concatenate(
                    [
                        dot(vt[role, 0:HEAD_DIM, :], weights[:, 0:rows], NN),
                        dot(vt[role, HEAD_DIM:width, :], weights[:, rows : 2 * rows], NN),
                    ],
                    axis=0,
                )
            )
        row_sum, out = reduce(jnp.add, sums), reduce(jnp.add, outs)
        if group > 0:
            fade = jnp.exp(old - m)
            row_sum = row_sum + total[...] * fade
            out = out + acc[...] * by_head(fade)
        peak[...] = m
        peaks[group] = m
        total[...] = row_sum
        acc[...] = out

    def back_queries(h):
        cols = slice(h * rows, h * rows + rows)
        feats = slice(h * HEAD_DIM, (h + 1) * HEAD_DIM)
        out = jnp.zeros((HEAD_DIM, rows), jnp.float32)
        factor = HEAD_DIM**-0.5 / total[:, cols]
        delta = stats[OWN, 8 + h : 9 + h, :]
        for group, roles in enumerate(GROUPS):
            scale = factor * jnp.exp(peaks[group, :, cols] - peak[:, cols])
            for role in roles:
                dp = dot(kv[role, 1], dmt[:, cols], NN)
                ds = (probs[role, :, cols].astype(jnp.float32) * (dp - delta)).astype(jnp.bfloat16)
                out = out + scale * dot(kt[role, feats, :], ds, NN)
        acc[feats, :] = out

    def key_weights(role):
        pen = penalty(f + offsets[role], f)
        for h in range(2):
            at = slice(h * rows, h * rows + rows)
            st = dot(km[at, :], qs[role], NT)
            key_probs[role, at, :] = jnp.exp(st - (stats[role, h : h + 1, :] + pen)).astype(jnp.bfloat16)

    def back_keys(role):
        for h in range(2):
            at = slice(h * rows, h * rows + rows)
            pt = key_probs[role, at, :]
            dpt = dot(vm[at, :], do[role], NT)
            dst = (pt.astype(jnp.float32) * (dpt - stats[role, 8 + h : 9 + h, :])).astype(jnp.bfloat16)
            gv = dot(pt, do[role], NN)
            gk = dot(dst, qs[role], NN)
            if role != OWN:
                gv = gv + gv_acc[at, :]
                gk = gk + gk_acc[at, :]
            gv_acc[at, :] = gv
            gk_acc[at, :] = gk

    loads[0].wait()
    g_all[z] = g_ref[...].T
    loads[1].wait()
    loads[2].wait()
    pl.semaphore_wait(barrier, SPAN - 1 + heads - 1 + QUARTERS - 1)

    def grad_edge(o):
        src = g_all.at[z, pl.ds(rows - RIM if o == 1 else 0, RIM)]
        return edge(src, mail, 0, o)

    for o in (1, -1):
        grad_edge(o).start()
    hops(g_all, g_s, g_r, (0, 1))
    for role in (UP, DOWN, PAIR):
        route(kv, kv_s, kv_r, role).start()
    loads[3].wait()
    qs[OWN] = (qs[OWN].astype(jnp.float32) * HEAD_DIM**-0.5).astype(jnp.bfloat16)
    head_columns(qs[OWN].T, qmt)
    loads[4].wait()
    mail[2 * RIM : MAIL - 1, :] = t_ref[...]
    mail[MAIL - 1 : MAIL, :] = jnp.zeros((1, width), jnp.bfloat16)
    loads[5].wait()
    for i in range(1, heads):
        weight(i).start()
    wcol[z, own_rows] = w_ref[own_rows, part(z)]
    grad_acc[...] = jnp.zeros_like(grad_acc)
    loads[6].wait()
    loads[7].wait()
    forward(0)

    for o in (1, -1):
        grad_edge(o).wait_recv()
    for i in range(1, heads):
        post(mail, mail_all, m_s, m_r, i).start()
    mail_all[z] = mail[...]
    route(kv, kv_s, kv_r, PAIR).wait_recv()
    hops(g_all, g_s, g_r, (2, 3))
    forward(1)
    head_rows(kv[OWN, 0], km)
    head_rows(kv[OWN, 1], vm)
    conv_group(z)
    arrive(g_all, g_s, g_r, (0, 1))
    hops(g_all, g_s, g_r, (4, 5, 6, 7))
    route(kv, kv_s, kv_r, UP).wait_recv()
    route(kv, kv_s, kv_r, DOWN).wait_recv()
    for role in (FAR,) + SECOND:
        route(kv, kv_s, kv_r, role).start()
    for role in FIRST:
        route(qs, q_s, q_r, role).start()
    forward(2)
    for i in range(1, heads):
        weight(i, True).wait_recv()
    for d in range(1, QUARTERS):
        quarter(d).start()
    for role in SECOND:
        route(kv, kv_s, kv_r, role).wait_recv()
    forward(3)
    route(kv, kv_s, kv_r, FAR).wait_recv()
    forward(4)

    attended = (acc[...] * by_head(1.0 / total[...])).astype(jnp.bfloat16)
    at_all[z] = attended
    hops(at_all, at_s, at_r, (0, 1))
    by_frame = attended.T
    ends[0:RIM, :] = by_frame[rows - RIM : rows, :]
    ends[RIM : 2 * RIM, :] = by_frame[0:RIM, :]

    def attended_edge(o):
        return edge(ends.at[pl.ds(0 if o == 1 else RIM, RIM)], rim, 1, o)

    for o in (1, -1):
        attended_edge(o).start()
    logsum = peak[...] + jnp.log(total[...])
    stats[OWN, 0:1, :] = logsum[:, 0:rows]
    stats[OWN, 1:2, :] = logsum[:, rows : 2 * rows]
    stats[OWN, 2:8, :] = jnp.zeros((6, rows), jnp.float32)
    for role in range(1, SPAN):
        direct(role, 0).start()

    arrive(g_all, g_s, g_r, (2, 3))
    for i in range(1, heads):
        posted(mail, mail_all, m_s, m_r, i).wait_recv()

    def near_groups(i, carry):
        conv_group(zrel(i - 2 + i // 2))
        return carry

    lax.fori_loop(0, 4, near_groups, 0)
    hops(at_all, at_s, at_r, (2, 3))
    for role in (UP, DOWN):
        route(qs, q_s, q_r, role).wait_recv()
    for role in SECOND:
        route(qs, q_s, q_r, role).start()
    key_weights(OWN)
    for role in range(SPAN):
        kt[role] = kv[role, 0].T
    for d in range(1, QUARTERS):
        quarter(d, True).wait_recv()
    for i in range(heads):
        wcol_t[:, i * width : (i + 1) * width] = wcol[i].T
    arrive(g_all, g_s, g_r, (4, 5, 6, 7))

    def far_groups(i, carry):
        conv_group(zrel(i + 3))
        return carry

    lax.fori_loop(0, 3, far_groups, 0)

    grad_t = grad_acc[...].astype(jnp.bfloat16)
    do[OWN] = grad_t.T
    for role in FIRST:
        route(do, do_s, do_r, role).start()
    product = grad_t.astype(jnp.float32) * at_all[z].astype(jnp.float32)
    stats[OWN, 8:9, :] = jnp.sum(product[0:HEAD_DIM, :], axis=0, keepdims=True)
    stats[OWN, 9:10, :] = jnp.sum(product[HEAD_DIM:width, :], axis=0, keepdims=True)
    stats[OWN, 10:16, :] = jnp.zeros((6, rows), jnp.float32)
    for role in range(1, SPAN):
        direct(role, 1).start()
    head_columns(grad_t, dmt)

    def ready(role):
        if role not in (OWN, UP, DOWN):
            route(qs, q_s, q_r, role).wait_recv()
        if role != OWN:
            direct(role, 0).wait_recv()
        key_weights(role)

    back_queries(0)
    for o in (1, -1):
        attended_edge(o).wait_recv()
    for i in range(1, heads):
        post(rim, rim_all, e_s, e_r, i).start()
    rim_all[z] = rim[...]
    back_queries(1)
    dq_ref[...] = acc[...].T.astype(jnp.bfloat16)
    stores = [
        pltpu.make_async_copy(src, dst, out_s.at[n])
        for n, (src, dst) in enumerate(
            ((dq_ref, dq_hbm), (dk_ref, dk_hbm), (dv_ref, dv_hbm), (co_ref, co_hbm))
        )
    ]
    stores[0].start()
    ready(PAIR)
    arrive(at_all, at_s, at_r, (0, 1))
    hops(at_all, at_s, at_r, (4, 5, 6, 7))
    ready(UP)
    ready(DOWN)
    for role in (UP, DOWN):
        route(do, do_s, do_r, role).wait_recv()
    for role in SECOND:
        route(do, do_s, do_r, role).start()
    ready(PAIR_UP)
    ready(PAIR_DOWN)
    ready(FAR)
    back_keys(OWN)
    for i in range(1, heads):
        posted(rim, rim_all, e_s, e_r, i).wait_recv()
    side = jnp.zeros((2 * RIM, width), jnp.float32)
    for i in range(heads):
        side = side + dot(rim_all[i], wcol[i], NN)
    side_ref[...] = side.astype(jnp.bfloat16)
    taps[...] = mail_all[z, 2 * RIM : MAIL, :].astype(jnp.float32)

    def keys_of(role):
        if role not in (UP, DOWN):
            route(do, do_s, do_r, role).wait_recv()
        direct(role, 1).wait_recv()
        back_keys(role)

    keys_of(PAIR)
    keys_of(UP)
    keys_of(DOWN)
    keys_of(PAIR_UP)
    keys_of(PAIR_DOWN)
    keys_of(FAR)
    dv_ref[...] = jnp.where(low, gv_acc[0:rows, :], gv_acc[rows : 2 * rows, :]).astype(jnp.bfloat16)
    dk_ref[...] = jnp.where(low, gk_acc[0:rows, :], gk_acc[rows : 2 * rows, :]).astype(jnp.bfloat16)
    stores[1].start()
    stores[2].start()

    arrive(at_all, at_s, at_r, range(2, len(HOPS)))
    gathered = at_all[...].reshape(heads * width, rows)
    mixed = dot(wcol_t[...], gathered, NN).T.astype(jnp.bfloat16)
    pad[RIM : RIM + rows, :] = mixed.astype(jnp.float32)
    conv(side_ref[0:RIM, :], side_ref[RIM : 2 * RIM, :], False, conv_tmp)
    co_ref[...] = conv_tmp[...].T
    stores[3].start()

    for o in (1, -1):
        grad_edge(o).wait_send()
        attended_edge(o).wait_send()
    for role in range(1, SPAN):
        route(kv, kv_s, kv_r, role).wait_send()
        route(qs, q_s, q_r, role).wait_send()
        route(do, do_s, do_r, role).wait_send()
        direct(role, 0).wait_send()
        direct(role, 1).wait_send()
    for i in range(1, heads):
        weight(i).wait_send()
        post(mail, mail_all, m_s, m_r, i).wait_send()
        post(rim, rim_all, e_s, e_r, i).wait_send()
    for d in range(1, QUARTERS):
        quarter(d).wait_send()
    for n in range(len(HOPS)):
        hop(g_all, g_s, g_r, n).wait_send()
        hop(at_all, at_s, at_r, n).wait_send()
    for store in stores:
        store.wait()


def copy_out(*refs):
    half = len(refs) // 2
    sources, targets, sems = refs[:half], refs[half : 2 * half], refs[-1]
    copies = [
        pltpu.make_async_copy(src, dst, sems.at[n]) for n, (src, dst) in enumerate(zip(sources, targets))
    ]
    for copy in copies:
        copy.start()
    for copy in copies:
        copy.wait()


def on_device(queries, keys, values, out_weight, conv_kernel, grad_out, pattern, counts):
    _, rows, width = queries.shape
    frames, heads = lax.axis_size("frame"), lax.axis_size("head")
    bf, f32 = jnp.bfloat16, jnp.float32
    block, tall = (rows, width), (width, rows)
    hbm = pl.BlockSpec(memory_space=pltpu.HBM)
    dma = pltpu.SemaphoreType.DMA
    vmem = pl.BlockSpec(memory_space=pltpu.VMEM)
    shapes = [
        jax.ShapeDtypeStruct(tall, bf),
        jax.ShapeDtypeStruct(block, bf),
        jax.ShapeDtypeStruct(block, bf),
        jax.ShapeDtypeStruct(block, bf),
    ]
    results = pl.pallas_call(
        partial(kernel, frames, heads),
        out_shape=shapes,
        in_specs=[hbm] * 8,
        out_specs=[hbm] * 4,
        scratch_shapes=[
            pltpu.VMEM(tall, bf),
            pltpu.VMEM(block, bf),
            pltpu.VMEM(block, bf),
            pltpu.VMEM(block, bf),
            pltpu.VMEM(out_weight.shape, bf),
            pltpu.VMEM(conv_kernel.shape, bf),
            pltpu.VMEM(tall, bf),
            pltpu.SMEM((pattern.shape[2], 1, frames), jnp.int32),
            pltpu.SMEM(counts.shape, jnp.int32),
            pltpu.VMEM((SPAN, 2) + block, bf),
            pltpu.VMEM((SPAN,) + tall, bf),
            pltpu.VMEM((SPAN,) + tall, bf),
            pltpu.VMEM((SPAN,) + block, bf),
            pltpu.VMEM((SPAN,) + block, bf),
            pltpu.VMEM((SPAN, 16, rows), f32),
            pltpu.VMEM((heads,) + block, bf),
            pltpu.VMEM((heads,) + tall, bf),
            pltpu.VMEM((MAIL, width), bf),
            pltpu.VMEM((heads, MAIL, width), bf),
            pltpu.VMEM((2 * RIM, width), bf),
            pltpu.VMEM((2 * RIM, width), bf),
            pltpu.VMEM((heads, 2 * RIM, width), bf),
            pltpu.VMEM((2 * RIM, width), bf),
            pltpu.VMEM((heads, width, width), bf),
            pltpu.VMEM((width, heads * width), bf),
            pltpu.VMEM(block, bf),
            pltpu.VMEM((rows + 2 * RIM, width), f32),
            pltpu.VMEM((2 * RIM, width), f32),
            pltpu.VMEM(tall, f32),
            pltpu.VMEM((width, 2 * rows), bf),
            pltpu.VMEM((width, 2 * rows), bf),
            pltpu.VMEM((2 * rows, width), bf),
            pltpu.VMEM((2 * rows, width), bf),
            pltpu.VMEM((SPAN, rows, 2 * rows), bf),
            pltpu.VMEM((SPAN, 2 * rows, rows), bf),
            pltpu.VMEM((len(GROUPS), 1, 2 * rows), f32),
            pltpu.VMEM((1, 2 * rows), f32),
            pltpu.VMEM((1, 2 * rows), f32),
            pltpu.VMEM(tall, f32),
            pltpu.VMEM((2 * rows, width), f32),
            pltpu.VMEM((2 * rows, width), f32),
            dma((8,)),
            dma((4,)),
        ]
        + [dma((SPAN,))] * 6
        + [dma((2, SPAN))] * 2
        + [dma((heads,))] * 2
        + [dma((QUARTERS,))] * 2
        + [dma((heads,))] * 8
        + [dma((2, 2))] * 2,
        compiler_params=pltpu.CompilerParams(
            collective_id=0, has_side_effects=True, vmem_limit_bytes=56 * 1024 * 1024
        ),
    )(
        queries.reshape(block),
        keys.reshape(block),
        values.reshape(block),
        out_weight,
        conv_kernel,
        grad_out.reshape(width, rows),
        jnp.transpose(pattern, (2, 0, 1)),
        counts,
    )
    conv_out, dq, dk, dv = pl.pallas_call(
        copy_out,
        out_shape=shapes,
        in_specs=[vmem] * 4,
        out_specs=[hbm] * 4,
        scratch_shapes=[dma((4,))],
    )(*results)
    return (
        conv_out.reshape(grad_out.shape),
        dq.reshape(queries.shape),
        dk.reshape(keys.shape),
        dv.reshape(values.shape),
    )


def solution(mesh):
    return jax.shard_map(
        on_device,
        mesh=mesh,
        in_specs=(
            P(None, "frame", "head"),
            P(None, "frame", "head"),
            P(None, "frame", "head"),
            P("head", None),
            P(None, "head"),
            P("head", None, "frame"),
            P(),
            P(),
        ),
        out_specs=(
            P("head", None, "frame"),
            P(None, "frame", "head"),
            P(None, "frame", "head"),
            P(None, "frame", "head"),
        ),
        check_vma=False,
    )
```

```python
from functools import partial, reduce

import jax
import jax.numpy as jnp
from jax import lax
from jax.experimental import pallas as pl
from jax.experimental.pallas import tpu as pltpu
from jax.sharding import PartitionSpec as P

HEAD_DIM = 64
KERNEL = 31
SPAN = 7
HUGE = 1e30
MESH = pl.DeviceIdType.MESH
RIM = 16
MAIL = 64
QUARTERS = 4

NT = (((1,), (1,)), ((), ()))
NN = (((1,), (0,)), ((), ()))

OWN, PAIR, UP, DOWN, PAIR_UP, PAIR_DOWN, FAR = range(SPAN)
GROUPS = ((OWN,), (PAIR,), (UP, DOWN), (PAIR_UP, PAIR_DOWN), (FAR,))


def dot(a, b, dims):
    return lax.dot_general(a, b, dims, preferred_element_type=jnp.float32)


def remote(src, dst, s, r, dev):
    return pltpu.make_async_remote_copy(
        src_ref=src, dst_ref=dst, send_sem=s, recv_sem=r, device_id=dev, device_id_type=MESH
    )


def kernel(
    frames,
    heads,
    q_hbm,
    k_hbm,
    v_hbm,
    w_hbm,
    t_hbm,
    g_hbm,
    pat_hbm,
    cnt_hbm,
    co_hbm,
    dq_hbm,
    dk_hbm,
    dv_hbm,
    co_ref,
    dq_ref,
    dk_ref,
    dv_ref,
    w_ref,
    t_ref,
    g_ref,
    pat_ref,
    cnt_ref,
    kv,
    kt,
    vt,
    qs,
    do,
    stats,
    g_all,
    at_all,
    mail,
    mail_all,
    ends,
    rim,
    rim_all,
    side_ref,
    wcol,
    wcol_t,
    conv_tmp,
    pad,
    taps,
    grad_acc,
    qmt,
    dmt,
    km,
    vm,
    probs,
    key_probs,
    peaks,
    peak,
    total,
    acc,
    gk_acc,
    gv_acc,
    in_s,
    out_s,
    kv_s,
    kv_r,
    q_s,
    q_r,
    do_s,
    do_r,
    st_s,
    st_r,
    w_s,
    w_r,
    x_s,
    x_r,
    g_s,
    g_r,
    at_s,
    at_r,
    m_s,
    m_r,
    e_s,
    e_r,
    h_s,
    h_r,
):
    f = lax.axis_index("frame")
    z = lax.axis_index("head")
    rows, width = kv.shape[2], kv.shape[3]
    odd = lax.rem(f, 2)
    sign = 2 * odd - 1

    def fdev(o):
        return (lax.rem(f + o + frames, frames), z)

    def zrel(i):
        return lax.rem(z + i + heads, heads)

    def part(index, size=width, start=0):
        return pl.ds(pl.multiple_of(index * width + start, size), size)

    offsets = (0, -sign, 2, -2, 2 - sign, -2 - sign, 3 * sign)

    barrier = pltpu.get_barrier_semaphore()
    for o in offsets[1:]:
        pl.semaphore_signal(barrier, inc=1, device_id=fdev(o), device_id_type=MESH)
    for i in range(1, heads):
        pl.semaphore_signal(barrier, inc=1, device_id=(f, zrel(i)), device_id_type=MESH)
    for d in range(1, QUARTERS):
        pl.semaphore_signal(barrier, inc=1, device_id=fdev(d * (frames // QUARTERS)), device_id_type=MESH)

    loads = [
        pltpu.make_async_copy(src, dst, in_s.at[n])
        for n, (src, dst) in enumerate(
            (
                (g_hbm, g_ref),
                (k_hbm, kv.at[OWN, 0]),
                (v_hbm, kv.at[OWN, 1]),
                (q_hbm, qs.at[OWN]),
                (t_hbm, t_ref),
                (w_hbm, w_ref),
                (pat_hbm, pat_ref),
                (cnt_hbm, cnt_ref),
            )
        )
    ]
    for load in loads:
        load.start()

    def route(buf, s, r, role):
        src, o = {
            PAIR: (OWN, -sign),
            DOWN: (OWN, 2),
            UP: (OWN, -2),
            FAR: (UP + odd, sign) if buf is kv else (OWN, 3 * sign),
            PAIR_UP: (UP, -sign),
            PAIR_DOWN: (DOWN, -sign),
        }[role]
        return remote(buf.at[src], buf.at[role], s.at[role], r.at[role], fdev(o))

    FIRST, SECOND = (UP, DOWN, PAIR, FAR), (PAIR_UP, PAIR_DOWN)

    def direct(role, which):
        o = {
            PAIR: -sign,
            DOWN: 2,
            UP: -2,
            PAIR_DOWN: 2 - sign,
            PAIR_UP: -2 - sign,
            FAR: 3 * sign,
        }[role]
        at = pl.ds(8 * which, 8)
        return remote(
            stats.at[OWN, at], stats.at[role, at], st_s.at[which, role], st_r.at[which, role], fdev(o)
        )

    def edge(src, dst, which, o):
        side = 0 if o == 1 else 1
        at = pl.ds(side * RIM, RIM)
        return remote(src, dst.at[at], h_s.at[which, side], h_r.at[which, side], fdev(o))

    def post(src, dst, s, r, i):
        return remote(src, dst.at[z], s.at[i], r.at[z], (f, zrel(i)))

    def posted(src, dst, s, r, i):
        origin = zrel(i)
        return remote(src, dst.at[origin], s.at[i], r.at[origin], (f, origin))

    stride, share = frames // QUARTERS, width // QUARTERS
    own_rows = pl.ds(pl.multiple_of((f // stride) * share, share), share)

    def weight(i, arrived=False):
        there = zrel(i)
        if arrived:
            return remote(wcol.at[there, own_rows], wcol.at[there, own_rows], w_s.at[i], w_r.at[there], (f, there))
        return remote(w_ref.at[own_rows, part(there)], wcol.at[z, own_rows], w_s.at[i], w_r.at[z], (f, there))

    def quarter(d, arrived=False):
        back = lax.rem(f // stride + QUARTERS - d, QUARTERS) if arrived else f // stride
        at = pl.ds(pl.multiple_of(back * share, share), share)
        return remote(wcol.at[:, at], wcol.at[:, at], x_s.at[d], x_r.at[d], fdev(d * stride))

    HOPS = ((0, 2), (0, -2), (0, 1), (0, -1), (-2, 1), (2, -1), (-2, 2), (2, -2))

    def hop(buf, s, r, n, arrived=False):
        origin, target = HOPS[n]
        slot = zrel(origin - target if arrived else origin)
        block = buf.at[slot]
        if n >= 6:
            half = buf.shape[1] // 2
            block = buf.at[slot, pl.ds(half * (n - 6), half)]
        return remote(block, block, s.at[n], r.at[n], (f, zrel(target)))

    def hops(buf, s, r, which):
        for n in which:
            hop(buf, s, r, n).start()

    def arrive(buf, s, r, which):
        for n in which:
            hop(buf, s, r, n, True).wait_recv()

    def penalty(query_block, key_block):
        inside = (query_block >= 0) & (query_block < frames) & (key_block >= 0) & (key_block < frames)
        safe = lax.rem(query_block + frames, frames)
        number = cnt_ref[0, safe]
        hit = False
        for entry in range(pat_ref.shape[0]):
            hit = hit | ((pat_ref[entry, 0, safe] == key_block) & (entry < number))
        return jnp.where(inside & hit, 0.0, HUGE)

    def conv(left, right, flip, out):
        pad[0:RIM, :] = jnp.where(f > 0, left.astype(jnp.float32), 0.0)
        pad[RIM + rows : 2 * RIM + rows, :] = jnp.where(f < frames - 1, right.astype(jnp.float32), 0.0)
        step = 64
        for c in range(rows // step):
            total_c = jnp.zeros((step, width), jnp.float32)
            for t in range(KERNEL):
                tap = KERNEL - 1 - t if flip else t
                total_c = total_c + taps[tap : tap + 1, :] * pad[c * step + t + 1 : c * step + t + 1 + step, :]
            out[c * step : c * step + step, :] = total_c.astype(jnp.bfloat16)

    def conv_group(group):
        pad[RIM : RIM + rows, :] = g_all[group].astype(jnp.float32)
        taps[...] = mail_all[group, 2 * RIM : MAIL, :].astype(jnp.float32)
        conv(mail_all[group, 0:RIM, :], mail_all[group, RIM : 2 * RIM, :], True, conv_tmp)
        grad_acc[...] += dot(w_ref[:, part(group)], conv_tmp[...], NT)

    def head_columns(x, dst):
        dst[0:HEAD_DIM, 0:rows] = x[0:HEAD_DIM, :]
        dst[HEAD_DIM:width, rows : 2 * rows] = x[HEAD_DIM:width, :]
        dst[0:HEAD_DIM, rows : 2 * rows] = jnp.zeros((HEAD_DIM, rows), jnp.bfloat16)
        dst[HEAD_DIM:width, 0:rows] = jnp.zeros((HEAD_DIM, rows), jnp.bfloat16)

    low = lax.broadcasted_iota(jnp.int32, (rows, width), 1) < HEAD_DIM

    def head_rows(x, dst):
        x = x.astype(jnp.float32)
        dst[0:rows, :] = jnp.where(low, x, 0.0).astype(jnp.bfloat16)
        dst[rows : 2 * rows, :] = jnp.where(low, 0.0, x).astype(jnp.bfloat16)

    def by_head(row):
        return jnp.concatenate(
            [
                jnp.broadcast_to(row[:, 0:rows], (HEAD_DIM, rows)),
                jnp.broadcast_to(row[:, rows : 2 * rows], (HEAD_DIM, rows)),
            ],
            axis=0,
        )

    def forward(group):
        roles = GROUPS[group]
        for role in roles:
            vt[role] = kv[role, 1].T
        scores = [dot(kv[role, 0], qmt[...], NN) for role in roles]
        pens = [penalty(f, f + offsets[role]) for role in roles]
        m = reduce(
            jnp.maximum, [jnp.max(s, axis=0, keepdims=True) - pen for s, pen in zip(scores, pens)]
        )
        if group > 0:
            old = peak[...]
            m = jnp.maximum(old, m)
        sums, outs = [], []
        for role, s, pen in zip(roles, scores, pens):
            p = jnp.exp(s - (m + pen))
            sums.append(jnp.sum(p, axis=0, keepdims=True))
            weights = p.astype(jnp.bfloat16)
            probs[role] = weights
            outs.append(
                jnp.concatenate(
                    [
                        dot(vt[role, 0:HEAD_DIM, :], weights[:, 0:rows], NN),
                        dot(vt[role, HEAD_DIM:width, :], weights[:, rows : 2 * rows], NN),
                    ],
                    axis=0,
                )
            )
        row_sum, out = reduce(jnp.add, sums), reduce(jnp.add, outs)
        if group > 0:
            fade = jnp.exp(old - m)
            row_sum = row_sum + total[...] * fade
            out = out + acc[...] * by_head(fade)
        peak[...] = m
        peaks[group] = m
        total[...] = row_sum
        acc[...] = out

    def back_queries(h):
        cols = slice(h * rows, h * rows + rows)
        feats = slice(h * HEAD_DIM, (h + 1) * HEAD_DIM)
        out = jnp.zeros((HEAD_DIM, rows), jnp.float32)
        factor = HEAD_DIM**-0.5 / total[:, cols]
        delta = stats[OWN, 8 + h : 9 + h, :]
        for group, roles in enumerate(GROUPS):
            scale = factor * jnp.exp(peaks[group, :, cols] - peak[:, cols])
            for role in roles:
                dp = dot(kv[role, 1], dmt[:, cols], NN)
                ds = (probs[role, :, cols].astype(jnp.float32) * (dp - delta)).astype(jnp.bfloat16)
                out = out + scale * dot(kt[role, feats, :], ds, NN)
        acc[feats, :] = out

    def key_weights(role):
        pen = penalty(f + offsets[role], f)
        for h in range(2):
            at = slice(h * rows, h * rows + rows)
            st = dot(km[at, :], qs[role], NT)
            key_probs[role, at, :] = jnp.exp(st - (stats[role, h : h + 1, :] + pen)).astype(jnp.bfloat16)

    def back_keys(role):
        for h in range(2):
            at = slice(h * rows, h * rows + rows)
            pt = key_probs[role, at, :]
            dpt = dot(vm[at, :], do[role], NT)
            dst = (pt.astype(jnp.float32) * (dpt - stats[role, 8 + h : 9 + h, :])).astype(jnp.bfloat16)
            gv = dot(pt, do[role], NN)
            gk = dot(dst, qs[role], NN)
            if role != OWN:
                gv = gv + gv_acc[at, :]
                gk = gk + gk_acc[at, :]
            gv_acc[at, :] = gv
            gk_acc[at, :] = gk

    loads[0].wait()
    g_all[z] = g_ref[...].T
    loads[1].wait()
    loads[2].wait()
    pl.semaphore_wait(barrier, SPAN - 1 + heads - 1 + QUARTERS - 1)

    def grad_edge(o):
        src = g_all.at[z, pl.ds(rows - RIM if o == 1 else 0, RIM)]
        return edge(src, mail, 0, o)

    for o in (1, -1):
        grad_edge(o).start()
    hops(g_all, g_s, g_r, (0, 1))
    for role in (UP, DOWN, PAIR):
        route(kv, kv_s, kv_r, role).start()
    loads[3].wait()
    qs[OWN] = (qs[OWN].astype(jnp.float32) * HEAD_DIM**-0.5).astype(jnp.bfloat16)
    head_columns(qs[OWN].T, qmt)
    loads[4].wait()
    mail[2 * RIM : MAIL - 1, :] = t_ref[...]
    mail[MAIL - 1 : MAIL, :] = jnp.zeros((1, width), jnp.bfloat16)
    loads[5].wait()
    for i in range(1, heads):
        weight(i).start()
    wcol[z, own_rows] = w_ref[own_rows, part(z)]
    grad_acc[...] = jnp.zeros_like(grad_acc)
    loads[6].wait()
    loads[7].wait()
    forward(0)

    for o in (1, -1):
        grad_edge(o).wait_recv()
    for i in range(1, heads):
        post(mail, mail_all, m_s, m_r, i).start()
    mail_all[z] = mail[...]
    route(kv, kv_s, kv_r, PAIR).wait_recv()
    hops(g_all, g_s, g_r, (2, 3))
    forward(1)
    head_rows(kv[OWN, 0], km)
    head_rows(kv[OWN, 1], vm)
    conv_group(z)
    arrive(g_all, g_s, g_r, (0, 1))
    hops(g_all, g_s, g_r, (4, 5, 6, 7))
    route(kv, kv_s, kv_r, UP).wait_recv()
    route(kv, kv_s, kv_r, DOWN).wait_recv()
    for role in (FAR,) + SECOND:
        route(kv, kv_s, kv_r, role).start()
    for role in FIRST:
        route(qs, q_s, q_r, role).start()
    forward(2)
    for i in range(1, heads):
        weight(i, True).wait_recv()
    for d in range(1, QUARTERS):
        quarter(d).start()
    for role in SECOND:
        route(kv, kv_s, kv_r, role).wait_recv()
    forward(3)
    route(kv, kv_s, kv_r, FAR).wait_recv()
    forward(4)

    attended = (acc[...] * by_head(1.0 / total[...])).astype(jnp.bfloat16)
    at_all[z] = attended
    hops(at_all, at_s, at_r, (0, 1))
    by_frame = attended.T
    ends[0:RIM, :] = by_frame[rows - RIM : rows, :]
    ends[RIM : 2 * RIM, :] = by_frame[0:RIM, :]

    def attended_edge(o):
        return edge(ends.at[pl.ds(0 if o == 1 else RIM, RIM)], rim, 1, o)

    for o in (1, -1):
        attended_edge(o).start()
    logsum = peak[...] + jnp.log(total[...])
    stats[OWN, 0:1, :] = logsum[:, 0:rows]
    stats[OWN, 1:2, :] = logsum[:, rows : 2 * rows]
    stats[OWN, 2:8, :] = jnp.zeros((6, rows), jnp.float32)
    for role in range(1, SPAN):
        direct(role, 0).start()

    arrive(g_all, g_s, g_r, (2, 3))
    for i in range(1, heads):
        posted(mail, mail_all, m_s, m_r, i).wait_recv()

    def near_groups(i, carry):
        conv_group(zrel(i - 2 + i // 2))
        return carry

    lax.fori_loop(0, 4, near_groups, 0)
    hops(at_all, at_s, at_r, (2, 3))
    for role in (UP, DOWN):
        route(qs, q_s, q_r, role).wait_recv()
    for role in SECOND:
        route(qs, q_s, q_r, role).start()
    key_weights(OWN)
    for role in range(SPAN):
        kt[role] = kv[role, 0].T
    for d in range(1, QUARTERS):
        quarter(d, True).wait_recv()
    for i in range(heads):
        wcol_t[:, i * width : (i + 1) * width] = wcol[i].T
    arrive(g_all, g_s, g_r, (4, 5, 6, 7))

    def far_groups(i, carry):
        conv_group(zrel(i + 3))
        return carry

    lax.fori_loop(0, 3, far_groups, 0)

    grad_t = grad_acc[...].astype(jnp.bfloat16)
    do[OWN] = grad_t.T
    for role in FIRST:
        route(do, do_s, do_r, role).start()
    product = grad_t.astype(jnp.float32) * at_all[z].astype(jnp.float32)
    stats[OWN, 8:9, :] = jnp.sum(product[0:HEAD_DIM, :], axis=0, keepdims=True)
    stats[OWN, 9:10, :] = jnp.sum(product[HEAD_DIM:width, :], axis=0, keepdims=True)
    stats[OWN, 10:16, :] = jnp.zeros((6, rows), jnp.float32)
    for role in range(1, SPAN):
        direct(role, 1).start()
    head_columns(grad_t, dmt)

    def ready(role):
        if role not in (OWN, UP, DOWN):
            route(qs, q_s, q_r, role).wait_recv()
        if role != OWN:
            direct(role, 0).wait_recv()
        key_weights(role)

    back_queries(0)
    for o in (1, -1):
        attended_edge(o).wait_recv()
    for i in range(1, heads):
        post(rim, rim_all, e_s, e_r, i).start()
    rim_all[z] = rim[...]
    back_queries(1)
    dq_ref[...] = acc[...].T.astype(jnp.bfloat16)
    stores = [
        pltpu.make_async_copy(src, dst, out_s.at[n])
        for n, (src, dst) in enumerate(
            ((dq_ref, dq_hbm), (dk_ref, dk_hbm), (dv_ref, dv_hbm), (co_ref, co_hbm))
        )
    ]
    stores[0].start()
    ready(PAIR)
    arrive(at_all, at_s, at_r, (0, 1))
    hops(at_all, at_s, at_r, (4, 5, 6, 7))
    ready(UP)
    ready(DOWN)
    for role in (UP, DOWN):
        route(do, do_s, do_r, role).wait_recv()
    for role in SECOND:
        route(do, do_s, do_r, role).start()
    ready(PAIR_UP)
    ready(PAIR_DOWN)
    ready(FAR)
    back_keys(OWN)
    for i in range(1, heads):
        posted(rim, rim_all, e_s, e_r, i).wait_recv()
    side = jnp.zeros((2 * RIM, width), jnp.float32)
    for i in range(heads):
        side = side + dot(rim_all[i], wcol[i], NN)
    side_ref[...] = side.astype(jnp.bfloat16)
    taps[...] = mail_all[z, 2 * RIM : MAIL, :].astype(jnp.float32)

    def keys_of(role):
        if role not in (UP, DOWN):
            route(do, do_s, do_r, role).wait_recv()
        direct(role, 1).wait_recv()
        back_keys(role)

    keys_of(PAIR)
    keys_of(UP)
    keys_of(DOWN)
    keys_of(PAIR_UP)
    keys_of(PAIR_DOWN)
    keys_of(FAR)
    dv_ref[...] = jnp.where(low, gv_acc[0:rows, :], gv_acc[rows : 2 * rows, :]).astype(jnp.bfloat16)
    dk_ref[...] = jnp.where(low, gk_acc[0:rows, :], gk_acc[rows : 2 * rows, :]).astype(jnp.bfloat16)
    stores[1].start()
    stores[2].start()

    arrive(at_all, at_s, at_r, range(2, len(HOPS)))
    gathered = at_all[...].reshape(heads * width, rows)
    mixed = dot(wcol_t[...], gathered, NN).T.astype(jnp.bfloat16)
    pad[RIM : RIM + rows, :] = mixed.astype(jnp.float32)
    conv(side_ref[0:RIM, :], side_ref[RIM : 2 * RIM, :], False, conv_tmp)
    co_ref[...] = conv_tmp[...].T
    stores[3].start()

    for o in (1, -1):
        grad_edge(o).wait_send()
        attended_edge(o).wait_send()
    for role in range(1, SPAN):
        route(kv, kv_s, kv_r, role).wait_send()
        route(qs, q_s, q_r, role).wait_send()
        route(do, do_s, do_r, role).wait_send()
        direct(role, 0).wait_send()
        direct(role, 1).wait_send()
    for i in range(1, heads):
        weight(i).wait_send()
        post(mail, mail_all, m_s, m_r, i).wait_send()
        post(rim, rim_all, e_s, e_r, i).wait_send()
    for d in range(1, QUARTERS):
        quarter(d).wait_send()
    for n in range(len(HOPS)):
        hop(g_all, g_s, g_r, n).wait_send()
        hop(at_all, at_s, at_r, n).wait_send()
    for store in stores:
        store.wait()


def copy_out(*refs):
    sources, targets, held = refs[0:4], refs[4:8], refs[8:12]
    in_sems, out_sems = refs[12:]
    loads = [pltpu.make_async_copy(sources[n], held[n], in_sems.at[n]) for n in range(4)]
    stores = [pltpu.make_async_copy(held[n], targets[n], out_sems.at[n]) for n in range(4)]
    for load in loads:
        load.start()
    for load, store in zip(loads, stores):
        load.wait()
        store.start()
    for store in stores:
        store.wait()


def on_device(queries, keys, values, out_weight, conv_kernel, grad_out, pattern, counts):
    _, rows, width = queries.shape
    frames, heads = lax.axis_size("frame"), lax.axis_size("head")
    bf, f32 = jnp.bfloat16, jnp.float32
    block, tall = (rows, width), (width, rows)
    hbm = pl.BlockSpec(memory_space=pltpu.HBM)
    dma = pltpu.SemaphoreType.DMA
    shapes = [
        jax.ShapeDtypeStruct(tall, bf),
        jax.ShapeDtypeStruct(block, bf),
        jax.ShapeDtypeStruct(block, bf),
        jax.ShapeDtypeStruct(block, bf),
    ]
    results = pl.pallas_call(
        partial(kernel, frames, heads),
        out_shape=shapes,
        in_specs=[hbm] * 8,
        out_specs=[hbm] * 4,
        scratch_shapes=[
            pltpu.VMEM(tall, bf),
            pltpu.VMEM(block, bf),
            pltpu.VMEM(block, bf),
            pltpu.VMEM(block, bf),
            pltpu.VMEM(out_weight.shape, bf),
            pltpu.VMEM(conv_kernel.shape, bf),
            pltpu.VMEM(tall, bf),
            pltpu.SMEM((pattern.shape[2], 1, frames), jnp.int32),
            pltpu.SMEM(counts.shape, jnp.int32),
            pltpu.VMEM((SPAN, 2) + block, bf),
            pltpu.VMEM((SPAN,) + tall, bf),
            pltpu.VMEM((SPAN,) + tall, bf),
            pltpu.VMEM((SPAN,) + block, bf),
            pltpu.VMEM((SPAN,) + block, bf),
            pltpu.VMEM((SPAN, 16, rows), f32),
            pltpu.VMEM((heads,) + block, bf),
            pltpu.VMEM((heads,) + tall, bf),
            pltpu.VMEM((MAIL, width), bf),
            pltpu.VMEM((heads, MAIL, width), bf),
            pltpu.VMEM((2 * RIM, width), bf),
            pltpu.VMEM((2 * RIM, width), bf),
            pltpu.VMEM((heads, 2 * RIM, width), bf),
            pltpu.VMEM((2 * RIM, width), bf),
            pltpu.VMEM((heads, width, width), bf),
            pltpu.VMEM((width, heads * width), bf),
            pltpu.VMEM(block, bf),
            pltpu.VMEM((rows + 2 * RIM, width), f32),
            pltpu.VMEM((2 * RIM, width), f32),
            pltpu.VMEM(tall, f32),
            pltpu.VMEM((width, 2 * rows), bf),
            pltpu.VMEM((width, 2 * rows), bf),
            pltpu.VMEM((2 * rows, width), bf),
            pltpu.VMEM((2 * rows, width), bf),
            pltpu.VMEM((SPAN, rows, 2 * rows), bf),
            pltpu.VMEM((SPAN, 2 * rows, rows), bf),
            pltpu.VMEM((len(GROUPS), 1, 2 * rows), f32),
            pltpu.VMEM((1, 2 * rows), f32),
            pltpu.VMEM((1, 2 * rows), f32),
            pltpu.VMEM(tall, f32),
            pltpu.VMEM((2 * rows, width), f32),
            pltpu.VMEM((2 * rows, width), f32),
            dma((8,)),
            dma((4,)),
        ]
        + [dma((SPAN,))] * 6
        + [dma((2, SPAN))] * 2
        + [dma((heads,))] * 2
        + [dma((QUARTERS,))] * 2
        + [dma((heads,))] * 8
        + [dma((2, 2))] * 2,
        compiler_params=pltpu.CompilerParams(
            collective_id=0, has_side_effects=True, vmem_limit_bytes=56 * 1024 * 1024
        ),
    )(
        queries.reshape(block),
        keys.reshape(block),
        values.reshape(block),
        out_weight,
        conv_kernel,
        grad_out.reshape(width, rows),
        jnp.transpose(pattern, (2, 0, 1)),
        counts,
    )
    conv_out, dq, dk, dv = pl.pallas_call(
        copy_out,
        out_shape=shapes,
        in_specs=[hbm] * 4,
        out_specs=[hbm] * 4,
        scratch_shapes=[pltpu.VMEM(shape.shape, bf) for shape in shapes] + [dma((4,)), dma((4,))],
    )(*results)
    return (
        conv_out.reshape(grad_out.shape),
        dq.reshape(queries.shape),
        dk.reshape(keys.shape),
        dv.reshape(values.shape),
    )


def solution(mesh):
    return jax.shard_map(
        on_device,
        mesh=mesh,
        in_specs=(
            P(None, "frame", "head"),
            P(None, "frame", "head"),
            P(None, "frame", "head"),
            P("head", None),
            P(None, "head"),
            P("head", None, "frame"),
            P(),
            P(),
        ),
        out_specs=(
            P("head", None, "frame"),
            P(None, "frame", "head"),
            P(None, "frame", "head"),
            P(None, "frame", "head"),
        ),
        check_vma=False,
    )
```
